32 devices in a mesh: groups: 2 (over y), blk: 4 (over z), shard: 2 (over x), sub: 2 (over core).
Axes of the slice: x: 2, y: 2, z: 4, core: 2. Of those that a mesh axis runs over, the one named last changes fastest.
Arguments:
- head_table: float32 [4096, 400], P(('groups', 'blk', 'shard', 'sub')), parts along dimension 0, may hold values from -1.5 to 1.5
- head_accum: float32 [4096], P(('groups', 'blk', 'shard', 'sub')), parts along dimension 0, may hold values from 0.005 to 0.05
- tail_table: float32 [4096, 400], P(('groups', 'blk', 'shard', 'sub')), parts along dimension 0, may hold values from -1.5 to 1.5
- tail_accum: float32 [4096], P(('groups', 'blk', 'shard', 'sub')), parts along dimension 0, may hold values from 0.005 to 0.05
- relations: float32 [1536, 400], P('groups'), parts along dimension 0, may hold values from 0.5 to 1.5
- rel_accum: float32 [1536], P('groups'), parts along dimension 0, may hold values from 0.005 to 0.05
- head_ids: int32 [2, 8192], P(None, ('groups', 'blk', 'shard', 'sub')), parts along dimension 1, may hold values from 0 to 127
- tail_ids: int32 [2, 8192], P(None, ('groups', 'blk', 'shard', 'sub')), parts along dimension 1, may hold values from 0 to 127
- rel_ids: int32 [2, 8192], P(None, ('groups', 'blk', 'shard', 'sub')), parts along dimension 1, may hold values from 0 to 767, as said below
- neg_ids: int32 [2, 64, 128], P(None, ('groups', 'blk', 'shard', 'sub')), parts along dimension 1, may hold values from 0 to 127
Outputs:
- head_out: float32 [4096, 400], P(('groups', 'blk', 'shard', 'sub')), parts along dimension 0
- head_acc_out: float32 [4096], P(('groups', 'blk', 'shard', 'sub')), parts along dimension 0
- tail_out: float32 [4096, 400], P(('groups', 'blk', 'shard', 'sub')), parts along dimension 0
- tail_acc_out: float32 [4096], P(('groups', 'blk', 'shard', 'sub')), parts along dimension 0
- rel_out: float32 [1536, 400], P('groups'), parts along dimension 0
- rel_acc_out: float32 [1536], P('groups'), parts along dimension 0
The draws below stay inside these ranges and needn't reach their ends.
There are 2 independent parts, one for each index of `groups`. The reference program is written for one: setup_inputs(seed, part) draws one part's arguments, and reference() takes and returns one part's arrays. A program takes and returns all parts, laid end to end along the dimension named above; each array names one. Nothing has to cross between parts.
Inputs may be any that keep to these rules, and one draw needn't show every extreme that they name: `rel_ids`: relation type of each edge; about half of a slice's edges use 768 // 16 relations tied to that slice.
All inputs are finite; a program needn't handle non-finite values.
Results may differ from the reference program's by a relative error of at most 0.0001.
Values sent between devices are 32-bit elements; how exact they have to be, the bound alone decides.
No kernel may reach another device: no remote copies, remote signals or barrier semaphores. Data moves between devices by JAX's collectives and lax.ppermute only.
A program may use at most 64 MiB of HBM per device.

```python
import math
import jax
import jax.numpy as jnp
from jax import lax

D = 400
R_DEV = 128
E_DEV = 256
STRETCH = 128
NEG = 128
NREL = 768
STEPS = 2
DEVS = 16
ENT = 2048
EDGES = 4096
STRETCHES = 32
N_BLK = 4
N_SHARD = 2
N_SUB = 2


def draw_rel_ids(key, part):
    key = jax.random.fold_in(key, 11)
    first, second, third = jax.random.split(key, 3)
    span = NREL // DEVS
    spread = jax.random.randint(first, (STEPS, EDGES), 0, NREL)
    owner = (jnp.arange(EDGES, dtype=jnp.int32) // E_DEV)[None, :] * span
    tied = owner + jax.random.randint(second, (STEPS, EDGES), 0, span)
    coin = jax.random.randint(third, (STEPS, EDGES), 0, 2)
    return jnp.where(coin == 1, tied, spread).astype(jnp.int32)


def place_ends(entries, rng, smallest, high):
    dims = entries.shape
    place = [jax.random.randint(jax.random.fold_in(rng, axis), (), 0, dims[axis]) for axis in range(len(dims))]
    entries = entries.at[tuple(place)].set(smallest)
    longest = dims.index(max(dims))
    place[longest] = (place[longest] + 1) % dims[longest]
    return entries.at[tuple(place)].set(high)


def block_levels(key, extent, cuts, smallest, largest):
    factor_of = 1.0
    for position, parts in cuts:
        draws = jax.random.uniform(jax.random.fold_in(jax.random.fold_in(key, 6), position), (parts,), jnp.float32, smallest / len(cuts), largest / len(cuts))
        factor_of = factor_of * jnp.repeat(jnp.exp(draws), extent[position] // parts).reshape((-1,) + (1,) * (len(extent) - 1 - position))
    return factor_of


def gaussian(key, extent, scale, bound, shards=(), kind=jnp.bfloat16):
    drawn = jax.random.normal(key, extent, jnp.float32) * scale
    if len(shards) > 0:
        drawn = block_levels(key, extent, shards, -0.22, 0.18) * drawn
    return jnp.clip(drawn, min=-bound, max=bound).astype(kind)


def setup_inputs(seed: int = 0, part: int = 0) -> dict:
    key_list = jax.random.split(jax.random.key(seed), 11)
    part_keys = jax.random.split(jax.random.fold_in(key_list[10], part), 11)
    return {
        "head_table": gaussian(part_keys[0], (ENT, D), 0.2236, 1.5, ((0, 16),), jnp.float32),
        "head_accum": jnp.clip(jnp.exp(math.log(0.05) - 2.3025851 * jax.random.uniform(part_keys[1], (ENT,), jnp.float32) ** block_levels(part_keys[1], (ENT,), ((0, 16),), -0.2, 0.2)), 0.005, 0.05),
        "tail_table": gaussian(part_keys[2], (ENT, D), 0.2236, 1.5, ((0, 16),), jnp.float32),
        "tail_accum": jnp.clip(jnp.exp(math.log(0.05) - 2.3025851 * jax.random.uniform(part_keys[3], (ENT,), jnp.float32) ** block_levels(part_keys[3], (ENT,), ((0, 16),), -0.2, 0.2)), 0.005, 0.05),
        "relations": jnp.clip(1.0 + 0.1 * jax.random.normal(part_keys[4], (NREL, D), jnp.float32), 0.5, 1.5),
        "rel_accum": jnp.clip(jnp.exp(jax.random.uniform(part_keys[5], (NREL,), jnp.float32, math.log(0.005), math.log(0.05))), 0.005, 0.05),
        "head_ids": place_ends(jax.random.randint(part_keys[6], (STEPS, EDGES), 0, R_DEV), jax.random.fold_in(part_keys[6], 1), 0, R_DEV - 1).astype(jnp.int32),
        "tail_ids": place_ends(jax.random.randint(part_keys[7], (STEPS, EDGES), 0, R_DEV), jax.random.fold_in(part_keys[7], 1), 0, R_DEV - 1).astype(jnp.int32),
        "rel_ids": draw_rel_ids(jax.random.fold_in(jax.random.fold_in(key_list[10], part), 71), part),
        "neg_ids": place_ends(jax.random.randint(part_keys[9], (STEPS, STRETCHES, NEG), 0, R_DEV), jax.random.fold_in(part_keys[9], 1), 0, R_DEV - 1).astype(jnp.int32),
    }


HIGH = lax.Precision.HIGHEST
RATE = 0.1

def adagrad(weights, accum, grads):
    accum = accum + lax.optimization_barrier(jnp.mean(grads * grads, axis=-1))
    return (weights - RATE * grads / jnp.sqrt(accum)[..., None], accum)

def bucket_grads(left, right, rel_table, left_ids, right_ids, kinds, negative):
    width = left.shape[1]
    rows = left.shape[0]
    heads = left[left_ids]
    tails = right[right_ids]
    rel_rows = rel_table[kinds]
    query = heads * rel_rows
    pos = lax.optimization_barrier(jnp.sum(query * tails, axis=-1))
    count = negative.shape[0]
    qgroup = query.reshape(count, -1, width)
    negrows = right[negative]
    scores = jnp.einsum('cid,cjd->cij', qgroup, negrows, precision=HIGH)
    gpos = -jax.nn.sigmoid(-pos)
    gneg = jax.nn.sigmoid(scores) / negative.shape[1]
    gquery = gpos[:, None] * tails + jnp.einsum('cij,cjd->cid', gneg, negrows, precision=HIGH).reshape(-1, width)
    gnegrows = jnp.einsum('cij,cid->cjd', gneg, qgroup, precision=HIGH).reshape(-1, width)
    grad_left = jnp.zeros((rows, width), jnp.float32).at[left_ids].add(gquery * rel_rows)
    grad_right = jnp.zeros((rows, width), jnp.float32).at[right_ids].add(gpos[:, None] * query)
    grad_right = grad_right.at[negative.reshape(-1)].add(gnegrows)
    grad_rel = jnp.zeros(rel_table.shape, jnp.float32).at[kinds].add(gquery * heads)
    return (grad_left, grad_right, grad_rel)

def reference(head_table, head_accum, tail_table, tail_accum, relations, rel_accum, head_ids, tail_ids, rel_ids, neg_ids):
    lanes = N_SHARD * N_SUB
    heads = head_table.reshape(DEVS, R_DEV, D)
    hacc = head_accum.reshape(DEVS, R_DEV)
    tails = tail_table.reshape(DEVS, R_DEV, D)
    tacc = tail_accum.reshape(DEVS, R_DEV)
    slots = jnp.arange(DEVS, dtype=jnp.int32)
    rel_table, racc = (relations, rel_accum)
    pairing = slots
    for step in range(STEPS):
        pairing = (slots // lanes - step) % N_BLK * lanes + slots % lanes
        cur = tails[pairing]
        cur_acc = tacc[pairing]
        hid = head_ids[step].reshape(DEVS, E_DEV)
        tid = tail_ids[step].reshape(DEVS, E_DEV)
        kid = rel_ids[step].reshape(DEVS, E_DEV)
        nid = neg_ids[step].reshape(DEVS, E_DEV // STRETCH, NEG)

        def one_slice(items):
            return bucket_grads(items[0], items[1], rel_table, items[2], items[3], items[4], items[5])
        grad_left, grad_right, grad_rel = lax.map(one_slice, (heads, cur, hid, tid, kid, nid))
        heads, hacc = adagrad(heads, hacc, grad_left)
        cur, cur_acc = adagrad(cur, cur_acc, grad_right)
        tails = tails.at[pairing].set(cur)
        tacc = tacc.at[pairing].set(cur_acc)
        rel_table, racc = adagrad(rel_table, racc, lax.optimization_barrier(jnp.sum(grad_rel, axis=0)))
    held = tails[pairing].reshape(ENT, D)
    held_acc = tacc[pairing].reshape(ENT)
    return (heads.reshape(ENT, D), hacc.reshape(ENT), held, held_acc, rel_table, racc)
```

```python
import functools

import jax
import jax.numpy as jnp
from jax import lax
from jax.experimental import pallas as pl
from jax.experimental.pallas import tpu as pltpu
from jax.sharding import PartitionSpec as P

RATE = 0.1
AXES = ("blk", "shard", "sub")
LANES = 128
PIECES = 8
F32 = jnp.float32
BF16 = jnp.bfloat16


def halves(x):
    high = x.astype(BF16)
    return high, (x - high.astype(F32)).astype(BF16)


def nn(a, b):
    return lax.dot_general(a, b, (((1,), (0,)), ((), ())), preferred_element_type=F32)


def nt(a, b):
    return lax.dot_general(a, b, (((1,), (1,)), ((), ())), preferred_element_type=F32)


def times_selector(dot, x, selector):
    high, low = halves(x)
    rows = x.shape[0]
    both = dot(jnp.concatenate([high, low], axis=0), selector)
    return both[:rows] + both[rows:]


def times(dot, a, b):
    a_high, a_low = halves(a)
    b_high, b_low = halves(b)
    rows = a.shape[0]
    both = dot(jnp.concatenate([a_high, a_low], axis=0), b_high)
    return both[:rows] + (both[rows:] + dot(a_high, b_low))


def selector(ids, rows):
    return (lax.broadcasted_iota(jnp.int32, (rows, ids.shape[1]), 0) == ids).astype(F32)


def adagrad(weights, accum, grads):
    accum = accum + jnp.sum(grads * grads, axis=0, keepdims=True) * (1.0 / grads.shape[0])
    return weights - grads * (RATE / jnp.sqrt(accum)), accum


def bucket(left, right, rel, head_ids, tail_ids, kinds, negative):
    rows = left.shape[1]
    edges = head_ids.shape[1]
    count, negs = negative.shape
    head_sel = selector(head_ids, rows)
    tail_sel = selector(tail_ids, rows)
    kind_sel = selector(kinds, rel.shape[1]).astype(BF16)
    heads = times_selector(nn, left, head_sel.astype(BF16))
    rel_rows = times_selector(nn, rel, kind_sel)
    query = heads * rel_rows
    scores = times(nn, right.T, query)
    tiny = jnp.exp(-jnp.abs(scores))
    inverse = 1.0 / (1.0 + tiny)
    up = scores >= 0
    sig = jnp.where(up, 1.0, tiny) * inverse
    sig_minus = jnp.where(up, tiny, 1.0) * inverse
    named = []
    for c in range(count):
        hits = lax.broadcasted_iota(jnp.int32, (rows, negs), 0) == negative[c : c + 1]
        times_named = jnp.sum(hits.astype(F32), axis=1, keepdims=True) * (1.0 / negs)
        named.append(jnp.broadcast_to(times_named, (rows, edges // count)))
    weight = jnp.concatenate(named, axis=1) * sig - tail_sel * sig_minus
    grad_query = times(nn, right, weight)
    grad_right = times(nt, query, weight)
    grad_left = times_selector(nt, grad_query * rel_rows, head_sel.astype(BF16))
    return grad_left, grad_right, grad_query * heads, kind_sel


def put_rel_grad(terms, kind_sel, out_ref):
    width = terms.shape[0]
    grad = times_selector(nt, terms, kind_sel)
    blocks = grad.shape[1] // LANES
    for j in range(blocks):
        out_ref[width * j : width * (j + 1), :] = grad[:, LANES * j : LANES * (j + 1)]
    rest = out_ref.shape[0] - width * blocks
    if rest:
        out_ref[width * blocks :, :] = jnp.zeros((rest, LANES), F32)


def take_rel_grad(place_ref, mine_ref, other_ref, all_ref, width, blocks):
    square, core = place_ref[0], place_ref[1]
    for i in range(PIECES // 2):
        piece = jnp.bitwise_xor(square, i)
        all_ref[core * (PIECES // 2) + piece] = mine_ref[i]
        all_ref[(1 - core) * (PIECES // 2) + piece] = other_ref[i]
    flat = all_ref[...].reshape(-1, LANES)
    return jnp.concatenate([flat[width * j : width * (j + 1)] for j in range(blocks)], axis=1)


def first_kernel(
    left_ref, lacc_ref, right_ref, racc_ref, rel_ref, hid_ref, tid_ref, kid_ref, nid_ref,
    left_out, lacc_out, right_out, grad_out,
):
    left, right = left_ref[...], right_ref[...]
    width = left.shape[0]
    grad_left, grad_right, terms, kind_sel = bucket(
        left, right, rel_ref[...], hid_ref[0:1], tid_ref[0:1], kid_ref[0:1], nid_ref[0]
    )
    put_rel_grad(terms, kind_sel, grad_out)
    left_out[...], lacc_out[...] = adagrad(left, lacc_ref[...], grad_left)
    right, acc = adagrad(right, racc_ref[...], grad_right)
    right_out[:width] = right
    right_out[width:] = jnp.broadcast_to(acc, (8, acc.shape[1]))


def next_kernel(
    step,
    place_ref, left_ref, lacc_ref, right_ref, rel_ref, relacc_ref, mine_ref, other_ref,
    hid_ref, tid_ref, kid_ref, nid_ref,
    left_out, lacc_out, right_out, rel_out, relacc_out, grad_out,
    all_ref,
):
    left = left_ref[...]
    width = left.shape[0]
    rel = rel_ref[...]
    summed = take_rel_grad(place_ref, mine_ref, other_ref, all_ref, width, rel.shape[1] // LANES)
    rel, relacc = adagrad(rel, relacc_ref[...], summed)
    rel_out[...] = rel
    relacc_out[...] = relacc
    right = right_ref[:width]
    grad_left, grad_right, terms, kind_sel = bucket(
        left, right, rel,
        hid_ref[step : step + 1], tid_ref[step : step + 1], kid_ref[step : step + 1], nid_ref[step],
    )
    put_rel_grad(terms, kind_sel, grad_out)
    left_out[...], lacc_out[...] = adagrad(left, lacc_ref[...], grad_left)
    right, acc = adagrad(right, right_ref[width : width + 1], grad_right)
    right_out[:width] = right
    right_out[width:] = jnp.broadcast_to(acc, (8, acc.shape[1]))


def last_kernel(place_ref, rel_ref, relacc_ref, mine_ref, other_ref, rel_out, relacc_out, all_ref):
    rel = rel_ref[...]
    summed = take_rel_grad(place_ref, mine_ref, other_ref, all_ref, rel.shape[0], rel.shape[1] // LANES)
    rel_out[...], relacc_out[...] = adagrad(rel, relacc_ref[...], summed)


VMEM = pl.BlockSpec(memory_space=pltpu.VMEM)
SMEM = pl.BlockSpec(memory_space=pltpu.SMEM)
PARAMS = pltpu.CompilerParams(vmem_limit_bytes=40 * 1024 * 1024)


def call(kernel, outs, placed, scratch=()):
    return pl.pallas_call(
        kernel,
        out_shape=[jax.ShapeDtypeStruct(shape, F32) for shape in outs],
        in_specs=[SMEM] * placed[0] + [VMEM] * placed[1],
        out_specs=[VMEM] * len(outs),
        scratch_shapes=[pltpu.VMEM(shape, F32) for shape in scratch],
        compiler_params=PARAMS,
    )


def swap(x, sizes, blk=0, shard=0, sub=0):
    n_blk, n_shard, n_sub = sizes

    def number(b, k, u):
        return (b * n_shard + k) * n_sub + u

    route = [
        (number(b, k, u), number(b ^ blk, k ^ shard, u ^ sub))
        for b in range(n_blk)
        for k in range(n_shard)
        for u in range(n_sub)
    ]
    return lax.ppermute(x, AXES, route)


def gray(i):
    return jnp.bitwise_and(jnp.bitwise_xor(i, i >> 1), 1)


def sum_pieces(grad, sizes, square, core):
    half = PIECES // 2
    pieces = grad.reshape(2, half, -1, LANES)
    kept = lax.dynamic_index_in_dim(pieces, core, 0, keepdims=False)
    sent = lax.dynamic_index_in_dim(pieces, 1 - core, 0, keepdims=False)
    kept = kept + swap(sent, sizes, sub=1)

    def piece(i):
        return lax.dynamic_index_in_dim(kept, jnp.bitwise_xor(square, i), 0, keepdims=False)

    total = piece(0)
    for i in range(1, half):
        total = total + swap(piece(i), sizes, blk=i & 1, shard=i >> 1)
    reach = 4
    while reach <= sizes[0]:
        total = total + swap(total, sizes, blk=reach - 1)
        reach *= 2
    reach = 4
    while reach <= sizes[1]:
        total = total + swap(total, sizes, shard=reach - 1)
        reach *= 2
    mine = jnp.stack([total] + [swap(total, sizes, blk=i & 1, shard=i >> 1) for i in range(1, half)])
    return mine, swap(mine, sizes, sub=1)


def from_behind(block, axis):
    n = lax.axis_size(axis)
    return lax.ppermute(block, axis, [((i - 1) % n, i) for i in range(n)])


def shards(
    head_table, head_accum, tail_table, tail_accum, relations, rel_accum, head_ids, tail_ids, rel_ids, neg_ids
):
    sizes = tuple(lax.axis_size(a) for a in AXES)
    steps = head_ids.shape[0]
    rows, width = head_table.shape
    kinds = relations.shape[0]
    core = lax.axis_index("sub")
    square = gray(lax.axis_index("shard")) * 2 + gray(lax.axis_index("blk"))
    place = jnp.stack([square, core]).astype(jnp.int32)
    tile = 8 * PIECES
    grad_rows = -(-(width * kinds // LANES) // tile) * tile
    pieces = (PIECES, grad_rows // PIECES, LANES)

    left, lacc = head_table.T, head_accum[None]
    rel, relacc = relations.T, rel_accum[None]
    ids = (head_ids, tail_ids, rel_ids, neg_ids)
    step_outs = [(width, rows), (1, rows), (width + 8, rows)]
    rel_outs = [(width, kinds), (1, kinds)]
    left, lacc, right, grad = call(first_kernel, step_outs + [(grad_rows, LANES)], (0, 9))(
        left, lacc, tail_table.T, tail_accum[None], rel, *ids
    )
    for step in range(1, steps):
        right = from_behind(right, "blk")
        mine, other = sum_pieces(grad, sizes, square, core)
        left, lacc, right, rel, relacc, grad = call(
            functools.partial(next_kernel, step), step_outs + rel_outs + [(grad_rows, LANES)], (1, 11), [pieces]
        )(place, left, lacc, right, rel, relacc, mine, other, *ids)
    mine, other = sum_pieces(grad, sizes, square, core)
    rel, relacc = call(last_kernel, rel_outs, (1, 4), [pieces])(place, rel, relacc, mine, other)
    return (left.T, lacc[0], right[:width].T, right[width], rel.T, relacc[0])


def solution(mesh):
    every = ("groups", "blk", "shard", "sub")
    return jax.shard_map(
        shards,
        mesh=mesh,
        in_specs=(
            P(every, None),
            P(every),
            P(every, None),
            P(every),
            P("groups", None),
            P("groups"),
            P(None, every),
            P(None, every),
            P(None, every),
            P(None, every, None),
        ),
        out_specs=(P(every, None), P(every), P(every, None), P(every), P("groups", None), P("groups")),
        check_vma=False,
    )
```

```python
import functools

import jax
import jax.numpy as jnp
from jax import lax
from jax.experimental import pallas as pl
from jax.experimental.pallas import tpu as pltpu
from jax.sharding import PartitionSpec as P

RATE = 0.1
AXES = ("blk", "shard", "sub")
LANES = 128
PIECES = 8
F32 = jnp.float32
BF16 = jnp.bfloat16


def halves(x):
    high = x.astype(BF16)
    return high, (x - high.astype(F32)).astype(BF16)


def nn(a, b):
    return lax.dot_general(a, b, (((1,), (0,)), ((), ())), preferred_element_type=F32)


def nt(a, b):
    return lax.dot_general(a, b, (((1,), (1,)), ((), ())), preferred_element_type=F32)


def times_selector(dot, x, selector):
    high, low = halves(x)
    rows = x.shape[0]
    both = dot(jnp.concatenate([high, low], axis=0), selector)
    return both[:rows] + both[rows:]


def times(dot, a, b):
    a_high, a_low = halves(a)
    b_high, b_low = halves(b)
    rows = a.shape[0]
    both = dot(jnp.concatenate([a_high, a_low], axis=0), b_high)
    return both[:rows] + (both[rows:] + dot(a_high, b_low))


def selector(ids, rows):
    return (lax.broadcasted_iota(jnp.int32, (rows, ids.shape[1]), 0) == ids).astype(F32)


def adagrad(weights, accum, grads):
    accum = accum + jnp.sum(grads * grads, axis=0, keepdims=True) * (1.0 / grads.shape[0])
    return weights - grads * (RATE / jnp.sqrt(accum)), accum


def bucket(left, right, rel, head_ids, tail_ids, kinds, negative):
    rows = left.shape[1]
    edges = head_ids.shape[1]
    count, negs = negative.shape
    head_sel = selector(head_ids, rows)
    tail_sel = selector(tail_ids, rows)
    kind_sel = selector(kinds, rel.shape[1]).astype(BF16)
    heads = times_selector(nn, left, head_sel.astype(BF16))
    rel_rows = times_selector(nn, rel, kind_sel)
    query = heads * rel_rows
    scores = times(nn, right.T, query)
    tiny = jnp.exp(-jnp.abs(scores))
    inverse = 1.0 / (1.0 + tiny)
    up = scores >= 0
    sig = jnp.where(up, 1.0, tiny) * inverse
    sig_minus = jnp.where(up, tiny, 1.0) * inverse
    named = []
    for c in range(count):
        hits = lax.broadcasted_iota(jnp.int32, (rows, negs), 0) == negative[c : c + 1]
        times_named = jnp.sum(hits.astype(F32), axis=1, keepdims=True) * (1.0 / negs)
        named.append(jnp.broadcast_to(times_named, (rows, edges // count)))
    weight = jnp.concatenate(named, axis=1) * sig - tail_sel * sig_minus
    grad_query = times(nn, right, weight)
    grad_right = times(nt, query, weight)
    grad_left = times_selector(nt, grad_query * rel_rows, head_sel.astype(BF16))
    return grad_left, grad_right, grad_query * heads, kind_sel


def put_rel_grad(terms, kind_sel, out_ref):
    width = terms.shape[0]
    grad = times_selector(nt, terms, kind_sel)
    blocks = grad.shape[1] // LANES
    for j in range(blocks):
        out_ref[width * j : width * (j + 1), :] = grad[:, LANES * j : LANES * (j + 1)]
    rest = out_ref.shape[0] - width * blocks
    if rest:
        out_ref[width * blocks :, :] = jnp.zeros((rest, LANES), F32)


def take_rel_grad(place_ref, piece_refs, all_ref, width, blocks):
    square, core = place_ref[0], place_ref[1]
    half = PIECES // 2
    for i in range(half):
        piece = jnp.bitwise_xor(square, i)
        all_ref[core * half + piece] = piece_refs[i][...]
        all_ref[(1 - core) * half + piece] = piece_refs[half + i][...]
    flat = all_ref[...].reshape(-1, LANES)
    return jnp.concatenate([flat[width * j : width * (j + 1)] for j in range(blocks)], axis=1)


def put_packed(out_ref, right, acc):
    width = right.shape[0]
    out_ref[:width] = right
    out_ref[width:] = jnp.broadcast_to(acc, (8, acc.shape[1]))


def first_kernel(*refs):
    given, (left_out, lacc_out, right_out, grad_out), held, sems = refs[:9], refs[9:13], refs[13:22], refs[22]
    copies = [pltpu.make_async_copy(a, b, sems.at[i]) for i, (a, b) in enumerate(zip(given, held))]
    for copy in copies:
        copy.start()
    for copy in copies:
        copy.wait()
    left_ref, lacc_ref, right_ref, racc_ref, rel_ref, hid_ref, tid_ref, kid_ref, nid_ref = held
    left, right = left_ref[...], right_ref[...]
    grad_left, grad_right, terms, kind_sel = bucket(
        left, right, rel_ref[...], hid_ref[0:1], tid_ref[0:1], kid_ref[0:1], nid_ref[0]
    )
    put_rel_grad(terms, kind_sel, grad_out)
    left_out[...], lacc_out[...] = adagrad(left, lacc_ref[...], grad_left)
    put_packed(right_out, *adagrad(right, racc_ref[...], grad_right))


def next_kernel(step, last, place_ref, left_ref, lacc_ref, right_ref, rel_ref, relacc_ref, *refs):
    piece_refs, (hid_ref, tid_ref, kid_ref, nid_ref) = refs[:PIECES], refs[PIECES : PIECES + 4]
    left_out, lacc_out, right_out, *racc_out, rel_out, relacc_out, grad_out, all_ref = refs[PIECES + 4 :]
    left = left_ref[...]
    width = left.shape[0]
    rel = rel_ref[...]
    summed = take_rel_grad(place_ref, piece_refs, all_ref, width, rel.shape[1] // LANES)
    rel, relacc = adagrad(rel, relacc_ref[...], summed)
    rel_out[...] = rel
    relacc_out[...] = relacc
    right = right_ref[:width]
    grad_left, grad_right, terms, kind_sel = bucket(
        left, right, rel,
        hid_ref[step : step + 1], tid_ref[step : step + 1], kid_ref[step : step + 1], nid_ref[step],
    )
    put_rel_grad(terms, kind_sel, grad_out)
    left_out[...], lacc = adagrad(left, lacc_ref[...], grad_left)
    right, racc = adagrad(right, right_ref[width : width + 1], grad_right)
    if last:
        right_out[...] = right
        lacc_out[...], racc_out[0][...] = lacc[0], racc[0]
    else:
        lacc_out[...] = lacc
        put_packed(right_out, right, racc)


def last_kernel(place_ref, rel_ref, relacc_ref, *refs):
    piece_refs, (rel_out, relacc_out, all_ref) = refs[:PIECES], refs[PIECES:]
    rel = rel_ref[...]
    summed = take_rel_grad(place_ref, piece_refs, all_ref, rel.shape[0], rel.shape[1] // LANES)
    rel_out[...], acc = adagrad(rel, relacc_ref[...], summed)
    relacc_out[...] = acc[0]


HBM = pl.BlockSpec(memory_space=pltpu.HBM)
VMEM = pl.BlockSpec(memory_space=pltpu.VMEM)
SMEM = pl.BlockSpec(memory_space=pltpu.SMEM)
PARAMS = pltpu.CompilerParams(vmem_limit_bytes=40 * 1024 * 1024)


def call(kernel, outs, placed, scratch=()):
    return pl.pallas_call(
        kernel,
        out_shape=[jax.ShapeDtypeStruct(shape, F32) for shape in outs],
        in_specs=[SMEM] * placed[0] + [VMEM] * placed[1],
        out_specs=[VMEM] * len(outs),
        scratch_shapes=[pltpu.VMEM(shape, F32) for shape in scratch],
        compiler_params=PARAMS,
    )


def swap(x, sizes, blk=0, shard=0, sub=0):
    n_blk, n_shard, n_sub = sizes

    def number(b, k, u):
        return (b * n_shard + k) * n_sub + u

    route = [
        (number(b, k, u), number(b ^ blk, k ^ shard, u ^ sub))
        for b in range(n_blk)
        for k in range(n_shard)
        for u in range(n_sub)
    ]
    return lax.ppermute(x, AXES, route)


def gray(i):
    return jnp.bitwise_and(jnp.bitwise_xor(i, i >> 1), 1)


def sum_pieces(grad, sizes, square, core, beside=()):
    half = PIECES // 2
    pieces = grad.reshape(2, half, -1, LANES)
    kept = lax.dynamic_index_in_dim(pieces, core, 0, keepdims=False)
    sent = lax.dynamic_index_in_dim(pieces, 1 - core, 0, keepdims=False)
    kept = kept + swap(sent, sizes, sub=1)

    def piece(i):
        return lax.dynamic_index_in_dim(kept, jnp.bitwise_xor(square, i), 0, keepdims=False)

    total = piece(0)
    got = [swap(piece(i), sizes, blk=i & 1, shard=i >> 1) for i in range(1, half)]
    got[1], beside = lax.optimization_barrier((got[1], beside))
    total = total + got[0] + got[1] + got[2]
    reach = 4
    while reach <= sizes[0]:
        total = total + swap(total, sizes, blk=reach - 1)
        reach *= 2
    reach = 4
    while reach <= sizes[1]:
        total = total + swap(total, sizes, shard=reach - 1)
        reach *= 2
    mine = [total] + [swap(total, sizes, blk=i & 1, shard=i >> 1) for i in range(1, half)]
    return mine + [swap(x, sizes, sub=1) for x in mine], beside


def from_behind(block, axis):
    n = lax.axis_size(axis)
    return lax.ppermute(block, axis, [((i - 1) % n, i) for i in range(n)])


def shards(
    head_table, head_accum, tail_table, tail_accum, relations, rel_accum, head_ids, tail_ids, rel_ids, neg_ids
):
    sizes = tuple(lax.axis_size(a) for a in AXES)
    steps = head_ids.shape[0]
    rows, width = head_table.shape
    kinds = relations.shape[0]
    core = lax.axis_index("sub")
    square = gray(lax.axis_index("shard")) * 2 + gray(lax.axis_index("blk"))
    place = jnp.stack([square, core]).astype(jnp.int32)
    tile = 8 * PIECES
    grad_rows = -(-(width * kinds // LANES) // tile) * tile
    pieces = (PIECES, grad_rows // PIECES, LANES)

    left, lacc = head_table.T, head_accum[None]
    rel, relacc = relations.T, rel_accum[None]
    ids = (head_ids, tail_ids, rel_ids, neg_ids)
    given = (left, lacc, tail_table.T, tail_accum[None], rel, *ids)
    step_outs = [(width, rows), (1, rows), (width + 8, rows)]
    last_outs = [(width, rows), (rows,), (width, rows), (rows,)]
    left, lacc, right, grad = pl.pallas_call(
        first_kernel,
        out_shape=[jax.ShapeDtypeStruct(shape, F32) for shape in step_outs + [(grad_rows, LANES)]],
        in_specs=[HBM] * len(given),
        out_specs=[VMEM] * 4,
        scratch_shapes=[pltpu.VMEM(x.shape, x.dtype) for x in given] + [pltpu.SemaphoreType.DMA((len(given),))],
        compiler_params=PARAMS,
    )(*[pltpu.with_memory_space_constraint(x, pltpu.HBM) for x in given])
    for step in range(1, steps):
        last = step + 1 == steps
        right = from_behind(right, "blk")
        summed, right = sum_pieces(grad, sizes, square, core, right)
        outs = (last_outs if last else step_outs) + [(width, kinds), (1, kinds), (grad_rows, LANES)]
        left, lacc, right, *racc, rel, relacc, grad = call(
            functools.partial(next_kernel, step, last), outs, (1, 9 + PIECES), [pieces]
        )(place, left, lacc, right, rel, relacc, *summed, *ids)
    summed, _ = sum_pieces(grad, sizes, square, core)
    rel, relacc = call(last_kernel, [(width, kinds), (kinds,)], (1, 2 + PIECES), [pieces])(place, rel, relacc, *summed)
    return (left.T, lacc, right.T, racc[0], rel.T, relacc)


def solution(mesh):
    every = ("groups", "blk", "shard", "sub")
    return jax.shard_map(
        shards,
        mesh=mesh,
        in_specs=(
            P(every, None),
            P(every),
            P(every, None),
            P(every),
            P("groups", None),
            P("groups"),
            P(None, every),
            P(None, every),
            P(None, every),
            P(None, every, None),
        ),
        out_specs=(P(every, None), P(every), P(every, None), P(every), P("groups", None), P("groups")),
        check_vma=False,
    )
```

```python
import functools
import math

import jax
import jax.numpy as jnp
from jax import lax
from jax.experimental import pallas as pl
from jax.experimental.pallas import tpu as pltpu
from jax.sharding import PartitionSpec as P

RATE = 0.1
AXES = ("blk", "shard", "sub")
LANES = 128
PIECES = 8
F32 = jnp.float32
BF16 = jnp.bfloat16


def halves(x):
    high = x.astype(BF16)
    return high, (x - high.astype(F32)).astype(BF16)


def nn(a, b):
    return lax.dot_general(a, b, (((1,), (0,)), ((), ())), preferred_element_type=F32)


def nt(a, b):
    return lax.dot_general(a, b, (((1,), (1,)), ((), ())), preferred_element_type=F32)


def times_selector(dot, x, selector):
    high, low = halves(x)
    rows = x.shape[0]
    both = dot(jnp.concatenate([high, low], axis=0), selector)
    return both[:rows] + both[rows:]


def times(dot, a, b):
    a_high, a_low = halves(a)
    b_high, b_low = halves(b)
    rows = a.shape[0]
    both = dot(jnp.concatenate([a_high, a_low], axis=0), b_high)
    return both[:rows] + (both[rows:] + dot(a_high, b_low))


def selector(ids, rows):
    return (lax.broadcasted_iota(jnp.int32, (rows, ids.shape[1]), 0) == ids).astype(F32)


def adagrad(weights, accum, grads):
    accum = accum + jnp.sum(grads * grads, axis=0, keepdims=True) * (1.0 / grads.shape[0])
    return weights - grads * (RATE / jnp.sqrt(accum)), accum


def score(right, rel_rows, heads, tail_ids, negative):
    rows = right.shape[1]
    count, negs = negative.shape
    query = heads * rel_rows
    scores = times(nn, right.T, query)
    tiny = jnp.exp(-jnp.abs(scores))
    inverse = 1.0 / (1.0 + tiny)
    up = scores >= 0
    sig = jnp.where(up, 1.0, tiny) * inverse
    sig_minus = jnp.where(up, tiny, 1.0) * inverse
    named = []
    for c in range(count):
        hits = lax.broadcasted_iota(jnp.int32, (rows, negs), 0) == negative[c : c + 1]
        share = jnp.sum(hits.astype(F32), axis=1, keepdims=True) * (1.0 / negs)
        named.append(jnp.broadcast_to(share, (rows, query.shape[1] // count)))
    weight = jnp.concatenate(named, axis=1) * sig - selector(tail_ids, rows) * sig_minus
    return query, weight


def cut(width):
    main = width // (8 * PIECES) * 8
    return main, width // PIECES - main


def put_terms(place_ref, terms, kinds, out_ref):
    square, core = place_ref[0], place_ref[1]
    width, edges = terms.shape
    half = PIECES // 2
    main, rest = cut(width)
    below = jnp.zeros((8 - rest - 1, LANES), F32)
    for c in range(PIECES):
        at = jnp.bitwise_xor(c // half, core) * half + jnp.bitwise_xor(c % half, square)
        last = main * PIECES + rest * c
        for j in range(edges // LANES):
            lanes = slice(LANES * j, LANES * (j + 1))
            top = (main + 8) * j
            out_ref[at, top : top + main] = terms[main * c : main * (c + 1), lanes]
            out_ref[at, top + main : top + main + 8] = jnp.concatenate(
                [terms[last : last + rest, lanes], kinds[:, lanes].astype(F32), below], axis=0
            )


def sum_terms(width, kinds, blocks_of_edges):
    main, rest = cut(width)
    total = None
    for i in range(0, len(blocks_of_edges), 2):
        pair = jnp.concatenate(blocks_of_edges[i : i + 2], axis=1)
        both = jnp.concatenate(halves(pair), axis=0)
        grad = nt(both, selector(pair[main + rest : main + rest + 1].astype(jnp.int32), kinds).astype(BF16))
        grad = grad[: main + 8] + grad[main + 8 :]
        total = grad if total is None else total + grad
    return total


def put_piece(grad, width, out_ref, before_ref=None):
    main, rest = cut(width)
    blocks = grad.shape[1] // LANES
    for j in range(blocks):
        lanes = slice(LANES * j, LANES * (j + 1))
        for rows, part in (
            (slice(main * j, main * (j + 1)), grad[:main, lanes]),
            (slice(main * blocks + rest * j, main * blocks + rest * (j + 1)), grad[main : main + rest, lanes]),
        ):
            out_ref[rows] = part if before_ref is None else before_ref[rows] + part
    end = (main + rest) * blocks
    out_ref[end:] = jnp.zeros((out_ref.shape[0] - end, LANES), F32)


def chip_kernel(width, kinds, own_ref, other_ref, out_ref):
    rows = cut(width)[0] + 8
    tiles = [ref[0, rows * j : rows * (j + 1)] for ref in (own_ref, other_ref) for j in range(ref.shape[1] // rows)]
    put_piece(sum_terms(width, kinds, tiles), width, out_ref)


def more_kernel(width, kinds, total_ref, terms_ref, out_ref):
    rows = cut(width)[0] + 8
    tiles = [terms_ref[rows * j : rows * (j + 1)] for j in range(terms_ref.shape[0] // rows)]
    put_piece(sum_terms(width, kinds, tiles), width, out_ref, total_ref)


def order_pieces(place_ref, piece_refs, all_ref):
    square, core = place_ref[0], place_ref[1]
    half = PIECES // 2
    for i in range(half):
        piece = jnp.bitwise_xor(square, i)
        all_ref[core * half + piece] = piece_refs[i][...]
        all_ref[(1 - core) * half + piece] = piece_refs[half + i][...]


def take_rel_grad(all_ref, j, width, blocks):
    main, rest = cut(width)
    first, last = main * j, main * blocks + rest * j
    return jnp.concatenate(
        [all_ref[c, first : first + main] for c in range(PIECES)]
        + [all_ref[c, last : last + rest] for c in range(PIECES)],
        axis=0,
    )


def next_accum(relacc_ref, all_ref, width):
    squares = []
    blocks = relacc_ref.shape[1] // LANES
    for j in range(blocks):
        grad = take_rel_grad(all_ref, j, width, blocks)
        squares.append(jnp.sum(grad * grad, axis=0, keepdims=True))
    accum = relacc_ref[...] + jnp.concatenate(squares, axis=1) * (1.0 / width)
    return accum, RATE / jnp.sqrt(accum)


def put_packed(out_ref, right, acc):
    width = right.shape[0]
    out_ref[:width] = right
    out_ref[width:] = jnp.broadcast_to(acc, (8, acc.shape[1]))


def first_kernel(place_ref, *refs):
    given, (right_out, terms_out, carry_out), held, sems = refs[:8], refs[8:11], refs[11:19], refs[19]
    copies = [pltpu.make_async_copy(a, b, sems.at[i]) for i, (a, b) in enumerate(zip(given, held))]
    for copy in copies:
        copy.start()
    hid_ref, tid_ref, kid_ref, nid_ref, left_ref, right_ref, racc_ref, rel_ref = held
    for copy in copies[:5]:
        copy.wait()
    head_sel = selector(hid_ref[0:1], left_ref.shape[1]).astype(BF16)
    kind_sel = selector(kid_ref[0:1], rel_ref.shape[1]).astype(BF16)
    heads = times_selector(nn, left_ref[...], head_sel)
    for copy in copies[5:]:
        copy.wait()
    right = right_ref[...]
    rel_rows = times_selector(nn, rel_ref[...], kind_sel)
    query, weight = score(right, rel_rows, heads, tid_ref[0:1], nid_ref[0])
    grad_query = times(nn, right, weight)
    put_terms(place_ref, grad_query * heads, kid_ref[0:1], terms_out)
    put_packed(right_out, *adagrad(right, racc_ref[...], times(nt, query, weight)))
    carry_out[...] = grad_query * rel_rows


def left_kernel(step, left_ref, lacc_ref, carry_ref, hid_ref, left_out, lacc_out, heads_out):
    rows = left_ref.shape[1]
    grad = times_selector(nt, carry_ref[...], selector(hid_ref[step : step + 1], rows).astype(BF16))
    left, lacc_out[...] = adagrad(left_ref[...], lacc_ref[...], grad)
    left_out[...] = left
    heads_out[...] = times_selector(nn, left, selector(hid_ref[step + 1 : step + 2], rows).astype(BF16))


def next_kernel(step, place_ref, heads_ref, right_ref, rel_ref, relacc_ref, *refs):
    piece_refs, (tid_ref, kid_ref, nid_ref) = refs[:PIECES], refs[PIECES : PIECES + 3]
    rel_out, relacc_out, terms_out, carry_out, query_out, weight_out, all_ref, split_ref = refs[PIECES + 3 :]
    width = heads_ref.shape[0]
    order_pieces(place_ref, piece_refs, all_ref)
    relacc_out[...], rate = next_accum(relacc_ref, all_ref, width)
    blocks = rel_ref.shape[1] // LANES
    for j in range(blocks):
        lanes = slice(LANES * j, LANES * (j + 1))
        rel = rel_ref[:, lanes] - take_rel_grad(all_ref, j, width, blocks) * rate[:, lanes]
        rel_out[:, lanes] = rel
        split_ref[:width, lanes], split_ref[width:, lanes] = halves(rel)
    kind_sel = selector(kid_ref[step : step + 1], rel_ref.shape[1]).astype(BF16)
    heads = heads_ref[...]
    both = nn(split_ref[...], kind_sel)
    rel_rows = both[:width] + both[width:]
    right = right_ref[:width]
    query, weight = score(right, rel_rows, heads, tid_ref[step : step + 1], nid_ref[step])
    grad_query = times(nn, right, weight)
    put_terms(place_ref, grad_query * heads, kid_ref[step : step + 1], terms_out)
    carry_out[...] = grad_query * rel_rows
    query_out[...] = query
    weight_out[...] = weight


def right_kernel(right_ref, query_ref, weight_ref, right_out):
    width = query_ref.shape[0]
    grad = times(nt, query_ref[...], weight_ref[...])
    put_packed(right_out, *adagrad(right_ref[:width], right_ref[width : width + 1], grad))


def update_kernel(
    step, left_ref, lacc_ref, carry_ref, hid_ref, right_ref, query_ref, weight_ref,
    left_out, lacc_out, right_out, racc_out,
):
    rows = left_ref.shape[1]
    grad = times_selector(nt, carry_ref[...], selector(hid_ref[step : step + 1], rows).astype(BF16))
    left_out[...], acc = adagrad(left_ref[...], lacc_ref[...], grad)
    lacc_out[...] = acc[0]
    width = left_ref.shape[0]
    grad = times(nt, query_ref[...], weight_ref[...])
    right_out[...], acc = adagrad(right_ref[:width], right_ref[width : width + 1], grad)
    racc_out[...] = acc[0]


def last_kernel(place_ref, rel_ref, relacc_ref, *refs):
    piece_refs, (rel_out, relacc_out, all_ref) = refs[:PIECES], refs[PIECES:]
    width = rel_ref.shape[0]
    order_pieces(place_ref, piece_refs, all_ref)
    accum, rate = next_accum(relacc_ref, all_ref, width)
    relacc_out[...] = accum[0]
    blocks = rel_ref.shape[1] // LANES
    for j in range(blocks):
        lanes = slice(LANES * j, LANES * (j + 1))
        rel_out[:, lanes] = rel_ref[:, lanes] - take_rel_grad(all_ref, j, width, blocks) * rate[:, lanes]


HBM = pl.BlockSpec(memory_space=pltpu.HBM)
VMEM = pl.BlockSpec(memory_space=pltpu.VMEM)
SMEM = pl.BlockSpec(memory_space=pltpu.SMEM)
PARAMS = pltpu.CompilerParams(vmem_limit_bytes=40 * 1024 * 1024)


def call(kernel, outs, scratch=(), smem=0, hbm_outs=(), name=None, flops=0):
    def run(*given):
        moved = sum(math.prod(x.shape) for x in given) + sum(math.prod(shape) for shape in outs)
        in_specs = [SMEM if i < smem else VMEM for i in range(len(given))]
        return pl.pallas_call(
            kernel,
            out_shape=[jax.ShapeDtypeStruct(shape, F32) for shape in outs],
            in_specs=in_specs,
            out_specs=[HBM if i in hbm_outs else VMEM for i in range(len(outs))],
            scratch_shapes=list(scratch),
            compiler_params=PARAMS,
            cost_estimate=pl.CostEstimate(flops=flops, bytes_accessed=4 * moved, transcendentals=0),
            name=name,
        )(*given)

    return run


def swap(x, sizes, blk=0, shard=0, sub=0):
    n_blk, n_shard, n_sub = sizes

    def number(b, k, u):
        return (b * n_shard + k) * n_sub + u

    route = [
        (number(b, k, u), number(b ^ blk, k ^ shard, u ^ sub))
        for b in range(n_blk)
        for k in range(n_shard)
        for u in range(n_sub)
    ]
    return lax.ppermute(x, AXES, route)


def gray(i):
    return jnp.bitwise_and(jnp.bitwise_xor(i, i >> 1), 1)


def sum_pieces(terms, sizes, width, kinds, beside=(), aside=()):
    half = PIECES // 2
    piece = (-(-(width // PIECES) * kinds // LANES // 8) * 8, LANES)
    other = swap(terms[half:], sizes, sub=1)
    got = [
        swap(jnp.concatenate([terms[i], other[i]], axis=0), sizes, blk=i & 1, shard=i >> 1) for i in range(1, half)
    ]
    got[1], beside = lax.optimization_barrier((got[1], beside))
    total = call(functools.partial(chip_kernel, width, kinds), [piece], name="chip_terms")(terms, other)[0]
    for more in (got[1], got[0], got[2]):
        total = call(functools.partial(more_kernel, width, kinds), [piece], name="more_terms")(total, more)[0]
    reach = 4
    while reach <= sizes[0]:
        total = total + swap(total, sizes, blk=reach - 1)
        reach *= 2
    reach = 4
    while reach <= sizes[1]:
        total = total + swap(total, sizes, shard=reach - 1)
        reach *= 2
    total, aside = lax.optimization_barrier((total, aside))
    mine = [total] + [swap(total, sizes, blk=i & 1, shard=i >> 1) for i in range(1, half)]
    return mine + [swap(x, sizes, sub=1) for x in mine], beside, aside


def from_behind(block, axis):
    n = lax.axis_size(axis)
    return lax.ppermute(block, axis, [((i - 1) % n, i) for i in range(n)])


def shards(
    head_table, head_accum, tail_table, tail_accum, relations, rel_accum, head_ids, tail_ids, rel_ids, neg_ids
):
    sizes = tuple(lax.axis_size(a) for a in AXES)
    steps = head_ids.shape[0]
    rows, width = head_table.shape
    kinds = relations.shape[0]
    core = lax.axis_index("sub")
    square = gray(lax.axis_index("shard")) * 2 + gray(lax.axis_index("blk"))
    place = jnp.stack([square, core]).astype(jnp.int32)

    left, lacc = head_table.T, head_accum[None]
    rel, relacc = relations.T, rel_accum[None]
    edges = head_ids.shape[1]
    table, state, each = (width, rows), (1, rows), (width, edges)
    cut_terms = (PIECES, edges // LANES * (cut(width)[0] + 8), LANES)
    given = (head_ids, tail_ids, rel_ids, neg_ids, left, tail_table.T, tail_accum[None], rel)
    right, terms, carry = pl.pallas_call(
        first_kernel,
        out_shape=[jax.ShapeDtypeStruct(shape, F32) for shape in [(width + 8, rows), cut_terms, each]],
        in_specs=[SMEM] + [HBM] * len(given),
        out_specs=[VMEM] * 3,
        scratch_shapes=[pltpu.VMEM(x.shape, x.dtype) for x in given] + [pltpu.SemaphoreType.DMA((len(given),))],
        compiler_params=PARAMS,
        name="first_step",
    )(place, *[pltpu.with_memory_space_constraint(x, pltpu.HBM) for x in given])
    all_pieces = pltpu.VMEM((PIECES, -(-(width // PIECES) * kinds // LANES // 8) * 8, LANES), F32)
    for step in range(1, steps):
        if step > 1:
            right = call(right_kernel, [(width + 8, rows)])(right, query, weight)
        right = from_behind(right, "blk")
        left, lacc, heads = call(functools.partial(left_kernel, step - 1), [table, state, each], name="left_update")(
            left, lacc, carry, head_ids
        )
        summed, right, (left, lacc, heads) = sum_pieces(terms, sizes, width, kinds, right, (left, lacc, heads))
        rel, relacc, terms, carry, query, weight = call(
            functools.partial(next_kernel, step),
            [(width, kinds), (1, kinds), cut_terms, each, each, (rows, edges)],
            [all_pieces, pltpu.VMEM((2 * width, kinds), BF16)],
            smem=1,
            name="next_step",
        )(place, heads, right, rel, relacc, *summed, tail_ids, rel_ids, neg_ids)
    updated = call(
        functools.partial(update_kernel, steps - 1), [table, (rows,), table, (rows,)], name="last_update"
    )(left, lacc, carry, head_ids, right, query, weight)
    summed, _, (left, lacc, right, racc) = sum_pieces(terms, sizes, width, kinds, aside=updated)
    rel, relacc = call(
        last_kernel,
        [(width, kinds), (kinds,)],
        [all_pieces],
        smem=1,
        name="last_relations",
    )(place, rel, relacc, *summed)
    return (left.T, lacc, right.T, racc, rel.T, relacc)


def solution(mesh):
    every = ("groups", "blk", "shard", "sub")
    return jax.shard_map(
        shards,
        mesh=mesh,
        in_specs=(
            P(every, None),
            P(every),
            P(every, None),
            P(every),
            P("groups", None),
            P("groups"),
            P(None, every),
            P(None, every),
            P(None, every),
            P(None, every, None),
        ),
        out_specs=(P(every, None), P(every), P(every, None), P(every), P("groups", None), P("groups")),
        check_vma=False,
    )
```

```python
import functools
import math

import jax
import jax.numpy as jnp
from jax import lax
from jax.experimental import pallas as pl
from jax.experimental.pallas import tpu as pltpu
from jax.sharding import PartitionSpec as P

RATE = 0.1
AXES = ("blk", "shard", "sub")
LANES = 128
PIECES = 8
F32 = jnp.float32
BF16 = jnp.bfloat16


def halves(x):
    high = x.astype(BF16)
    return high, (x - high.astype(F32)).astype(BF16)


def nn(a, b):
    return lax.dot_general(a, b, (((1,), (0,)), ((), ())), preferred_element_type=F32)


def nt(a, b):
    return lax.dot_general(a, b, (((1,), (1,)), ((), ())), preferred_element_type=F32)


def times_selector(dot, x, selector):
    high, low = halves(x)
    rows = x.shape[0]
    both = dot(jnp.concatenate([high, low], axis=0), selector)
    return both[:rows] + both[rows:]


def times(dot, a, b):
    a_high, a_low = halves(a)
    b_high, b_low = halves(b)
    rows = a.shape[0]
    both = dot(jnp.concatenate([a_high, a_low], axis=0), b_high)
    return both[:rows] + (both[rows:] + dot(a_high, b_low))


def selector(ids, rows):
    return (lax.broadcasted_iota(jnp.int32, (rows, ids.shape[1]), 0) == ids).astype(F32)


def adagrad(weights, accum, grads):
    accum = accum + jnp.sum(grads * grads, axis=0, keepdims=True) * (1.0 / grads.shape[0])
    return weights - grads * (RATE / jnp.sqrt(accum)), accum


def prepare(right, tail_ids, negative):
    rows = right.shape[1]
    count, negs = negative.shape
    named = []
    for c in range(count):
        hits = lax.broadcasted_iota(jnp.int32, (rows, negs), 0) == negative[c : c + 1]
        share = jnp.sum(hits.astype(F32), axis=1, keepdims=True) * (1.0 / negs)
        named.append(jnp.broadcast_to(share, (rows, tail_ids.shape[1] // count)))
    return jnp.concatenate(named, axis=1), selector(tail_ids, rows)


def split_times(dot, a_both, b):
    rows = a_both.shape[0] // 2
    b_high, b_low = halves(b)
    both = dot(a_both, b_high)
    return both[:rows] + (both[rows:] + dot(a_both[:rows], b_low))


def stack(x):
    return jnp.concatenate(halves(x), axis=0)


def score(right_turned, query, named, tail_sel):
    scores = split_times(nn, right_turned, query)
    tiny = jnp.exp(-jnp.abs(scores))
    inverse = 1.0 / (1.0 + tiny)
    up = scores >= 0
    sig = jnp.where(up, 1.0, tiny) * inverse
    sig_minus = jnp.where(up, tiny, 1.0) * inverse
    return named * sig - tail_sel * sig_minus


def cut(width):
    main = width // (8 * PIECES) * 8
    return main, width // PIECES - main


def piece_rows(width, kinds):
    return -(-(width // PIECES) * kinds // LANES // 8) * 8


def put_terms(place_ref, terms, kinds, out_ref):
    square, core = place_ref[0], place_ref[1]
    width, edges = terms.shape
    half = PIECES // 2
    main, rest = cut(width)
    below = jnp.zeros((8 - rest - 1, LANES), F32)
    for c in range(PIECES):
        at = jnp.bitwise_xor(c // half, core) * half + jnp.bitwise_xor(c % half, square)
        last = main * PIECES + rest * c
        for j in range(edges // LANES):
            lanes = slice(LANES * j, LANES * (j + 1))
            top = (main + 8) * j
            out_ref[at, top : top + main] = terms[main * c : main * (c + 1), lanes]
            out_ref[at, top + main : top + main + 8] = jnp.concatenate(
                [terms[last : last + rest, lanes], kinds[:, lanes].astype(F32), below], axis=0
            )


def sum_terms(width, kinds, blocks_of_edges):
    main, rest = cut(width)
    total = None
    for i in range(0, len(blocks_of_edges), 2):
        pair = jnp.concatenate(blocks_of_edges[i : i + 2], axis=1)
        both = jnp.concatenate(halves(pair), axis=0)
        grad = nt(both, selector(pair[main + rest : main + rest + 1].astype(jnp.int32), kinds).astype(BF16))
        grad = grad[: main + 8] + grad[main + 8 :]
        total = grad if total is None else total + grad
    return total


def put_piece(grad, width, out_ref, before_ref=None):
    main, rest = cut(width)
    blocks = grad.shape[1] // LANES
    for j in range(blocks):
        lanes = slice(LANES * j, LANES * (j + 1))
        for rows, part in (
            (slice(main * j, main * (j + 1)), grad[:main, lanes]),
            (slice(main * blocks + rest * j, main * blocks + rest * (j + 1)), grad[main : main + rest, lanes]),
        ):
            out_ref[rows] = part if before_ref is None else before_ref[rows] + part
    end = (main + rest) * blocks
    out_ref[end:] = jnp.zeros((out_ref.shape[0] - end, LANES), F32)


def chip_kernel(width, kinds, own_ref, other_ref, out_ref):
    rows = cut(width)[0] + 8
    tiles = [ref[0, rows * j : rows * (j + 1)] for ref in (own_ref, other_ref) for j in range(ref.shape[1] // rows)]
    put_piece(sum_terms(width, kinds, tiles), width, out_ref)


def more_kernel(width, kinds, total_ref, terms_ref, out_ref):
    rows = cut(width)[0] + 8
    tiles = [terms_ref[rows * j : rows * (j + 1)] for j in range(terms_ref.shape[0] // rows)]
    put_piece(sum_terms(width, kinds, tiles), width, out_ref, total_ref)


def order_pieces(place_ref, piece_refs, all_ref):
    square, core = place_ref[0], place_ref[1]
    half = PIECES // 2
    for i in range(half):
        piece = jnp.bitwise_xor(square, i)
        all_ref[core * half + piece] = piece_refs[i][...]
        all_ref[(1 - core) * half + piece] = piece_refs[half + i][...]


def take_rel_grad(all_ref, j, width, blocks):
    main, rest = cut(width)
    first, last = main * j, main * blocks + rest * j
    return jnp.concatenate(
        [all_ref[c, first : first + main] for c in range(PIECES)]
        + [all_ref[c, last : last + rest] for c in range(PIECES)],
        axis=0,
    )


def next_accum(relacc_ref, all_ref, width):
    squares = []
    blocks = relacc_ref.shape[1] // LANES
    for j in range(blocks):
        grad = take_rel_grad(all_ref, j, width, blocks)
        squares.append(jnp.sum(grad * grad, axis=0, keepdims=True))
    accum = relacc_ref[...] + jnp.concatenate(squares, axis=1) * (1.0 / width)
    return accum, RATE / jnp.sqrt(accum)


def put_packed(out_ref, right, acc):
    width = right.shape[0]
    out_ref[:width] = right
    out_ref[width:] = jnp.broadcast_to(acc, (8, acc.shape[1]))


def first_kernel(place_ref, *refs):
    given, (right_out, terms_out, carry_out), held, sems = refs[:8], refs[8:11], refs[11:19], refs[19]
    copies = [pltpu.make_async_copy(a, b, sems.at[i]) for i, (a, b) in enumerate(zip(given, held))]
    for copy in copies:
        copy.start()
    hid_ref, tid_ref, kid_ref, nid_ref, left_ref, right_ref, racc_ref, rel_ref = held
    for copy in copies[:5]:
        copy.wait()
    head_sel = selector(hid_ref[0:1], left_ref.shape[1]).astype(BF16)
    kind_sel = selector(kid_ref[0:1], rel_ref.shape[1]).astype(BF16)
    heads = times_selector(nn, left_ref[...], head_sel)
    for copy in copies[5:]:
        copy.wait()
    right = right_ref[...]
    rel_rows = times_selector(nn, rel_ref[...], kind_sel)
    query = heads * rel_rows
    weight = score(stack(right.T), query, *prepare(right, tid_ref[0:1], nid_ref[0]))
    grad_query = times(nn, right, weight)
    put_terms(place_ref, grad_query * heads, kid_ref[0:1], terms_out)
    put_packed(right_out, *adagrad(right, racc_ref[...], times(nt, query, weight)))
    carry_out[...] = grad_query * rel_rows


def ready_kernel(
    step, left_ref, lacc_ref, carry_ref, right_ref, rel_ref, relacc_ref, hid_ref, tid_ref, kid_ref, nid_ref,
    left_out, lacc_out, heads_out, turned_out, right_out, named_out, tail_out, kind_out, rows_out, state_out,
):
    width, rows = left_ref.shape
    grad = times_selector(nt, carry_ref[...], selector(hid_ref[step - 1 : step], rows).astype(BF16))
    left, lacc_out[...] = adagrad(left_ref[...], lacc_ref[...], grad)
    left_out[...] = left
    heads_out[...] = times_selector(nn, left, selector(hid_ref[step : step + 1], rows).astype(BF16))
    right = right_ref[:width]
    turned_out[...] = stack(right.T)
    right_out[...] = stack(right)
    named_out[...], tail_out[...] = prepare(right, tid_ref[step : step + 1], nid_ref[step])
    kind_sel = selector(kid_ref[step : step + 1], rel_ref.shape[1]).astype(BF16)
    kind_out[...] = kind_sel
    state = jnp.broadcast_to(relacc_ref[...], (8, rel_ref.shape[1]))
    rel_rows = times_selector(nn, jnp.concatenate([rel_ref[...], state], axis=0), kind_sel)
    rows_out[...] = rel_rows[:width]
    state_out[...] = rel_rows[width : width + 1]


def gather_pieces(piece_refs, kind_sel, width):
    main, rest = cut(width)
    blocks = kind_sel.shape[0] // LANES
    mains = [jnp.concatenate([ref[main * j : main * (j + 1)] for j in range(blocks)], axis=1) for ref in piece_refs]
    first = main * blocks
    rests = [
        jnp.concatenate([ref[first + rest * j : first + rest * (j + 1)] for j in range(blocks)], axis=1)
        for ref in piece_refs
    ]
    return times_selector(nn, jnp.concatenate(mains + rests, axis=0), kind_sel)


def gather_kernel(width, *refs):
    refs[-1][...] = gather_pieces(refs[:-2], refs[-2][...], width)


def next_kernel(step, place_ref, heads_ref, turned_ref, right_ref, named_ref, tail_ref, kind_ref, rows_ref, *refs):
    state_ref, mine_ref, piece_refs, kid_ref = refs[0], refs[1], refs[2 : 2 + PIECES // 2], refs[2 + PIECES // 2]
    terms_out, carry_out, query_out, weight_out, main_ref, rest_ref = refs[3 + PIECES // 2 :]
    heads = heads_ref[...]
    width = heads.shape[0]
    square, core = place_ref[0], place_ref[1]
    half = PIECES // 2
    main, rest = cut(width)
    theirs = gather_pieces(piece_refs, kind_ref[...], width)
    for first, columns in ((core * half, mine_ref[...]), ((1 - core) * half, theirs)):
        for i in range(half):
            at = first + jnp.bitwise_xor(square, i)
            last = main * half + rest * i
            main_ref[at] = columns[main * i : main * (i + 1)]
            rest_ref[at, :rest] = columns[last : last + rest]
    grad = jnp.concatenate([main_ref[c] for c in range(PIECES)] + [rest_ref[c, :rest] for c in range(PIECES)], axis=0)
    state = state_ref[...] + jnp.sum(grad * grad, axis=0, keepdims=True) * (1.0 / width)
    rel_rows = rows_ref[...] - grad * (RATE / jnp.sqrt(state))
    query = heads * rel_rows
    weight = score(turned_ref[...], query, named_ref[...], tail_ref[...])
    grad_query = split_times(nn, right_ref[...], weight)
    put_terms(place_ref, grad_query * heads, kid_ref[step : step + 1], terms_out)
    carry_out[...] = grad_query * rel_rows
    query_out[...] = query
    weight_out[...] = weight


def relations_kernel(place_ref, rel_ref, relacc_ref, *refs):
    piece_refs, (rel_out, relacc_out, all_ref) = refs[:PIECES], refs[PIECES:]
    width = rel_ref.shape[0]
    order_pieces(place_ref, piece_refs, all_ref)
    accum, rate = next_accum(relacc_ref, all_ref, width)
    relacc_out[...] = accum[0] if len(relacc_out.shape) == 1 else accum
    blocks = rel_ref.shape[1] // LANES
    for j in range(blocks):
        lanes = slice(LANES * j, LANES * (j + 1))
        rel_out[:, lanes] = rel_ref[:, lanes] - take_rel_grad(all_ref, j, width, blocks) * rate[:, lanes]


def right_kernel(right_ref, query_ref, weight_ref, right_out):
    width = query_ref.shape[0]
    grad = times(nt, query_ref[...], weight_ref[...])
    put_packed(right_out, *adagrad(right_ref[:width], right_ref[width : width + 1], grad))


def update_kernel(
    step, left_ref, lacc_ref, carry_ref, hid_ref, right_ref, query_ref, weight_ref,
    left_out, lacc_out, right_out, racc_out,
):
    rows = left_ref.shape[1]
    grad = times_selector(nt, carry_ref[...], selector(hid_ref[step : step + 1], rows).astype(BF16))
    left_out[...], acc = adagrad(left_ref[...], lacc_ref[...], grad)
    lacc_out[...] = acc[0]
    width = left_ref.shape[0]
    grad = times(nt, query_ref[...], weight_ref[...])
    right_out[...], acc = adagrad(right_ref[:width], right_ref[width : width + 1], grad)
    racc_out[...] = acc[0]


HBM = pl.BlockSpec(memory_space=pltpu.HBM)
VMEM = pl.BlockSpec(memory_space=pltpu.VMEM)
SMEM = pl.BlockSpec(memory_space=pltpu.SMEM)
PARAMS = pltpu.CompilerParams(vmem_limit_bytes=40 * 1024 * 1024)


def call(kernel, outs, scratch=(), smem=0, hbm_outs=(), name=None, flops=0):
    def run(*given):
        moved = sum(math.prod(x.shape) for x in given) + sum(math.prod(getattr(shape, "shape", shape)) for shape in outs)
        in_specs = [SMEM if i < smem else VMEM for i in range(len(given))]
        return pl.pallas_call(
            kernel,
            out_shape=[jax.ShapeDtypeStruct(shape, F32) if isinstance(shape, tuple) else shape for shape in outs],
            in_specs=in_specs,
            out_specs=[HBM if i in hbm_outs else VMEM for i in range(len(outs))],
            scratch_shapes=list(scratch),
            compiler_params=PARAMS,
            cost_estimate=pl.CostEstimate(flops=flops, bytes_accessed=4 * moved, transcendentals=0),
            name=name,
        )(*given)

    return run


def swap(x, sizes, blk=0, shard=0, sub=0):
    n_blk, n_shard, n_sub = sizes

    def number(b, k, u):
        return (b * n_shard + k) * n_sub + u

    route = [
        (number(b, k, u), number(b ^ blk, k ^ shard, u ^ sub))
        for b in range(n_blk)
        for k in range(n_shard)
        for u in range(n_sub)
    ]
    return lax.ppermute(x, AXES, route)


def gray(i):
    return jnp.bitwise_and(jnp.bitwise_xor(i, i >> 1), 1)


def sum_pieces(terms, sizes, width, kinds, beside=None, work=lambda _: ()):
    half = PIECES // 2
    piece = (piece_rows(width, kinds), LANES)
    sent = terms[half:]
    if beside is not None:
        sent, beside = lax.optimization_barrier((sent, beside))
        beside = from_behind(beside, "blk")
    other = swap(sent, sizes, sub=1)
    got = [
        swap(jnp.concatenate([terms[i], other[i]], axis=0), sizes, blk=i & 1, shard=i >> 1) for i in range(1, half)
    ]
    if beside is not None:
        got[1], beside = lax.optimization_barrier((got[1], beside))
    total = call(functools.partial(chip_kernel, width, kinds), [piece], name="chip_terms")(terms, other)[0]
    for more in (got[1], got[2], got[0]):
        total = call(functools.partial(more_kernel, width, kinds), [piece], name="more_terms")(total, more)[0]
    reach = 4
    while reach <= sizes[0]:
        total = total + swap(total, sizes, blk=reach - 1)
        reach *= 2
    reach = 4
    while reach <= sizes[1]:
        total = total + swap(total, sizes, shard=reach - 1)
        reach *= 2
    total, aside = lax.optimization_barrier((total, work(beside)))
    mine = [total] + [swap(total, sizes, blk=i & 1, shard=i >> 1) for i in range(1, half)]
    return mine + [swap(x, sizes, sub=1) for x in mine], beside, aside


def from_behind(block, axis):
    n = lax.axis_size(axis)
    return lax.ppermute(block, axis, [((i - 1) % n, i) for i in range(n)])


def shards(
    head_table, head_accum, tail_table, tail_accum, relations, rel_accum, head_ids, tail_ids, rel_ids, neg_ids
):
    sizes = tuple(lax.axis_size(a) for a in AXES)
    steps = head_ids.shape[0]
    rows, width = head_table.shape
    kinds = relations.shape[0]
    core = lax.axis_index("sub")
    square = gray(lax.axis_index("shard")) * 2 + gray(lax.axis_index("blk"))
    place = jnp.stack([square, core]).astype(jnp.int32)

    left, lacc = head_table.T, head_accum[None]
    rel, relacc = relations.T, rel_accum[None]
    edges = head_ids.shape[1]
    table, state, each = (width, rows), (1, rows), (width, edges)
    cut_terms = (PIECES, edges // LANES * (cut(width)[0] + 8), LANES)
    given = (head_ids, tail_ids, rel_ids, neg_ids, left, tail_table.T, tail_accum[None], rel)
    right, terms, carry = pl.pallas_call(
        first_kernel,
        out_shape=[jax.ShapeDtypeStruct(shape, F32) for shape in [(width + 8, rows), cut_terms, each]],
        in_specs=[SMEM] + [HBM] * len(given),
        out_specs=[VMEM] * 3,
        scratch_shapes=[pltpu.VMEM(x.shape, x.dtype) for x in given] + [pltpu.SemaphoreType.DMA((len(given),))],
        compiler_params=PARAMS,
        name="first_step",
    )(place, *[pltpu.with_memory_space_constraint(x, pltpu.HBM) for x in given])
    all_pieces = pltpu.VMEM((PIECES, piece_rows(width, kinds), LANES), F32)
    half = PIECES // 2
    main, rest = cut(width)

    def short(*shape):
        return jax.ShapeDtypeStruct(shape, BF16)

    def relations(rel, relacc, summed, shape, name):
        return call(relations_kernel, [(width, kinds), shape], [all_pieces], smem=1, name=name)(
            place, rel, relacc, *summed
        )

    summed = None
    for step in range(1, steps):
        if step > 1:
            right = call(right_kernel, [(width + 8, rows)])(right, query, weight)[0]

        def ready(right, step=step, rel=rel, relacc=relacc, summed=summed):
            if summed is not None:
                rel, relacc = relations(rel, relacc, summed, (1, kinds), "relations")
            outs = [table, state, each, short(2 * rows, width), short(2 * width, rows), (rows, edges), (rows, edges)]
            outs += [short(kinds, edges), each, (1, edges)]
            return rel, relacc, *call(functools.partial(ready_kernel, step), outs, name="ready")(
                left, lacc, carry, right, rel, relacc, head_ids, tail_ids, rel_ids, neg_ids
            )

        summed, right, (rel, relacc, left, lacc, heads, turned, both, named, tail_sel, kind_sel, rel_rows, rel_state) = (
            sum_pieces(terms, sizes, width, kinds, right, ready)
        )
        mine = call(functools.partial(gather_kernel, width), [(half * (main + rest), edges)], name="gather")(
            *summed[:half], kind_sel
        )[0]
        terms, carry, query, weight = call(
            functools.partial(next_kernel, step),
            [cut_terms, each, each, (rows, edges)],
            [pltpu.VMEM((PIECES, main, edges), F32), pltpu.VMEM((PIECES, 8, edges), F32)],
            smem=1,
            name="next_step",
        )(place, heads, turned, both, named, tail_sel, kind_sel, rel_rows, rel_state, mine, *summed[half:], rel_ids)

    def update(_):
        return *relations(rel, relacc, summed, (1, kinds), "relations"), *call(
            functools.partial(update_kernel, steps - 1), [table, (rows,), table, (rows,)], name="last_update"
        )(left, lacc, carry, head_ids, right, query, weight)

    last, _, (rel, relacc, left, lacc, right, racc) = sum_pieces(terms, sizes, width, kinds, work=update)
    rel, relacc = relations(rel, relacc, last, (kinds,), "last_relations")
    return (left.T, lacc, right.T, racc, rel.T, relacc)


def solution(mesh):
    every = ("groups", "blk", "shard", "sub")
    return jax.shard_map(
        shards,
        mesh=mesh,
        in_specs=(
            P(every, None),
            P(every),
            P(every, None),
            P(every),
            P("groups", None),
            P("groups"),
            P(None, every),
            P(None, every),
            P(None, every),
            P(None, every, None),
        ),
        out_specs=(P(every, None), P(every), P(every, None), P(every), P("groups", None), P("groups")),
        check_vma=False,
    )
```

```python
import functools
import math

import jax
import jax.numpy as jnp
from jax import lax
from jax.experimental import pallas as pl
from jax.experimental.pallas import tpu as pltpu
from jax.sharding import PartitionSpec as P

RATE = 0.1
AXES = ("blk", "shard", "sub")
LANES = 128
PIECES = 8
F32 = jnp.float32
BF16 = jnp.bfloat16


def halves(x):
    high = x.astype(BF16)
    return high, (x - high.astype(F32)).astype(BF16)


def nn(a, b):
    return lax.dot_general(a, b, (((1,), (0,)), ((), ())), preferred_element_type=F32)


def nt(a, b):
    return lax.dot_general(a, b, (((1,), (1,)), ((), ())), preferred_element_type=F32)


def times_selector(dot, x, selector):
    high, low = halves(x)
    rows = x.shape[0]
    both = dot(jnp.concatenate([high, low], axis=0), selector)
    return both[:rows] + both[rows:]


def times(dot, a, b):
    a_high, a_low = halves(a)
    b_high, b_low = halves(b)
    rows = a.shape[0]
    both = dot(jnp.concatenate([a_high, a_low], axis=0), b_high)
    return both[:rows] + (both[rows:] + dot(a_high, b_low))


def selector(ids, rows):
    return (lax.broadcasted_iota(jnp.int32, (rows, ids.shape[1]), 0) == ids).astype(F32)


def adagrad(weights, accum, grads):
    accum = accum + jnp.sum(grads * grads, axis=0, keepdims=True) * (1.0 / grads.shape[0])
    return weights - grads * (RATE / jnp.sqrt(accum)), accum


def prepare(right, tail_ids, negative):
    rows = right.shape[1]
    count, negs = negative.shape
    named = []
    for c in range(count):
        hits = lax.broadcasted_iota(jnp.int32, (rows, negs), 0) == negative[c : c + 1]
        share = jnp.sum(hits.astype(F32), axis=1, keepdims=True) * (1.0 / negs)
        named.append(jnp.broadcast_to(share, (rows, tail_ids.shape[1] // count)))
    return jnp.concatenate(named, axis=1), selector(tail_ids, rows)


def split_times(dot, a_both, b):
    rows = a_both.shape[0] // 2
    b_high, b_low = halves(b)
    both = dot(a_both, b_high)
    return both[:rows] + (both[rows:] + dot(a_both[:rows], b_low))


def stack(x):
    return jnp.concatenate(halves(x), axis=0)


def score(right_turned, query, named, tail_sel):
    scores = split_times(nn, right_turned, query)
    tiny = jnp.exp(-jnp.abs(scores))
    inverse = 1.0 / (1.0 + tiny)
    up = scores >= 0
    sig = jnp.where(up, 1.0, tiny) * inverse
    sig_minus = jnp.where(up, tiny, 1.0) * inverse
    return named * sig - tail_sel * sig_minus


def cut(width):
    main = width // (8 * PIECES) * 8
    return main, width // PIECES - main


def piece_rows(width, kinds):
    return -(-(width // PIECES) * kinds // LANES // 8) * 8


def term_rows(width, edges):
    return edges // LANES * cut(width)[0] + 8


def put_terms(place_ref, terms, kinds, out_ref):
    square, core = place_ref[0], place_ref[1]
    width, edges = terms.shape
    half = PIECES // 2
    main, rest = cut(width)
    tiles = [slice(LANES * j, LANES * (j + 1)) for j in range(edges // LANES)]
    ids = [kinds[:, lanes].astype(F32) for lanes in tiles]
    ids.append(jnp.zeros((8 - len(tiles) * (rest + 1), LANES), F32))
    for c in range(PIECES):
        at = jnp.bitwise_xor(c // half, core) * half + jnp.bitwise_xor(c % half, square)
        last = main * PIECES + rest * c
        for j, lanes in enumerate(tiles):
            out_ref[at, main * j : main * (j + 1)] = terms[main * c : main * (c + 1), lanes]
        out_ref[at, main * len(tiles) :] = jnp.concatenate(
            [terms[last : last + rest, lanes] for lanes in tiles] + ids, axis=0
        )


def turn(x, by):
    return [x[by:], x[:by]] if by else [x]


def sum_terms(width, kinds, parts):
    main, rest = cut(width)
    total = None
    for part in parts:
        tiles = part.shape[0] // main
        below = part[main * tiles :]
        each = [
            jnp.concatenate([part[main * j : main * (j + 1)]] + turn(below, rest * j), axis=0)
            for j in range(tiles)
        ]
        first = rest * tiles
        ids = jnp.concatenate([below[first + j : first + j + 1] for j in range(tiles)], axis=1)
        both = stack(jnp.concatenate(each, axis=1))
        grad = nt(both, selector(ids.astype(jnp.int32), kinds).astype(BF16))
        grad = grad[: main + 8] + grad[main + 8 :]
        total = grad if total is None else total + grad
    return total


def put_piece(grad, width, out_ref, before_ref=None):
    main, rest = cut(width)
    blocks = grad.shape[1] // LANES
    for j in range(blocks):
        lanes = slice(LANES * j, LANES * (j + 1))
        for rows, part in (
            (slice(main * j, main * (j + 1)), grad[:main, lanes]),
            (slice(main * blocks + rest * j, main * blocks + rest * (j + 1)), grad[main : main + rest, lanes]),
        ):
            out_ref[rows] = part if before_ref is None else before_ref[rows] + part
    end = (main + rest) * blocks
    out_ref[end:] = jnp.zeros((out_ref.shape[0] - end, LANES), F32)


def chip_kernel(width, kinds, own_ref, other_ref, out_ref):
    put_piece(sum_terms(width, kinds, [own_ref[0], other_ref[0]]), width, out_ref)


def more_kernel(width, kinds, total_ref, terms_ref, out_ref):
    rows = terms_ref.shape[0] // 2
    put_piece(sum_terms(width, kinds, [terms_ref[:rows], terms_ref[rows:]]), width, out_ref, total_ref)


def order_pieces(place_ref, piece_refs, all_ref):
    square, core = place_ref[0], place_ref[1]
    half = PIECES // 2
    for i in range(half):
        piece = jnp.bitwise_xor(square, i)
        all_ref[core * half + piece] = piece_refs[i][...]
        all_ref[(1 - core) * half + piece] = piece_refs[half + i][...]


def take_rel_grad(all_ref, j, width, blocks):
    main, rest = cut(width)
    first, last = main * j, main * blocks + rest * j
    return jnp.concatenate(
        [all_ref[c, first : first + main] for c in range(PIECES)]
        + [all_ref[c, last : last + rest] for c in range(PIECES)],
        axis=0,
    )


def next_accum(relacc_ref, all_ref, width):
    squares = []
    blocks = relacc_ref.shape[1] // LANES
    for j in range(blocks):
        grad = take_rel_grad(all_ref, j, width, blocks)
        squares.append(jnp.sum(grad * grad, axis=0, keepdims=True))
    accum = relacc_ref[...] + jnp.concatenate(squares, axis=1) * (1.0 / width)
    return accum, RATE / jnp.sqrt(accum)


def put_packed(out_ref, right, acc):
    width = right.shape[0]
    out_ref[:width] = right
    out_ref[width:] = jnp.broadcast_to(acc, (8, acc.shape[1]))


def first_kernel(place_ref, *refs):
    given, (right_out, terms_out, carry_out), held, sems = refs[:8], refs[8:11], refs[11:19], refs[19]
    copies = [pltpu.make_async_copy(a, b, sems.at[i]) for i, (a, b) in enumerate(zip(given, held))]
    for copy in copies:
        copy.start()
    hid_ref, tid_ref, kid_ref, nid_ref, left_ref, right_ref, racc_ref, rel_ref = held
    for copy in copies[:5]:
        copy.wait()
    head_sel = selector(hid_ref[0:1], left_ref.shape[1]).astype(BF16)
    kind_sel = selector(kid_ref[0:1], rel_ref.shape[1]).astype(BF16)
    heads = times_selector(nn, left_ref[...], head_sel)
    for copy in copies[5:]:
        copy.wait()
    right = right_ref[...]
    rel_rows = times_selector(nn, rel_ref[...], kind_sel)
    query = heads * rel_rows
    weight = score(stack(right.T), query, *prepare(right, tid_ref[0:1], nid_ref[0]))
    grad_query = times(nn, right, weight)
    put_terms(place_ref, grad_query * heads, kid_ref[0:1], terms_out)
    put_packed(right_out, *adagrad(right, racc_ref[...], times(nt, query, weight)))
    carry_out[...] = grad_query * rel_rows


def ready_kernel(
    step, left_ref, lacc_ref, carry_ref, right_ref, rel_ref, relacc_ref, hid_ref, tid_ref, kid_ref, nid_ref,
    left_out, lacc_out, heads_out, turned_out, right_out, named_out, tail_out, kind_out, rows_out, state_out,
):
    width, rows = left_ref.shape
    grad = times_selector(nt, carry_ref[...], selector(hid_ref[step - 1 : step], rows).astype(BF16))
    left, lacc_out[...] = adagrad(left_ref[...], lacc_ref[...], grad)
    left_out[...] = left
    heads_out[...] = times_selector(nn, left, selector(hid_ref[step : step + 1], rows).astype(BF16))
    right = right_ref[:width]
    turned_out[...] = stack(right.T)
    right_out[...] = stack(right)
    named_out[...], tail_out[...] = prepare(right, tid_ref[step : step + 1], nid_ref[step])
    kind_sel = selector(kid_ref[step : step + 1], rel_ref.shape[1]).astype(BF16)
    kind_out[...] = kind_sel
    state = jnp.broadcast_to(relacc_ref[...], (8, rel_ref.shape[1]))
    rel_rows = times_selector(nn, jnp.concatenate([rel_ref[...], state], axis=0), kind_sel)
    rows_out[...] = rel_rows[:width]
    state_out[...] = rel_rows[width : width + 1]


def gather_pieces(piece_refs, kind_sel, width):
    main, rest = cut(width)
    blocks = kind_sel.shape[0] // LANES
    mains = [jnp.concatenate([ref[main * j : main * (j + 1)] for j in range(blocks)], axis=1) for ref in piece_refs]
    first = main * blocks
    rests = [
        jnp.concatenate([ref[first + rest * j : first + rest * (j + 1)] for j in range(blocks)], axis=1)
        for ref in piece_refs
    ]
    return times_selector(nn, jnp.concatenate(mains + rests, axis=0), kind_sel)


def gather_kernel(width, *refs):
    refs[-1][...] = gather_pieces(refs[:-2], refs[-2][...], width)


def next_kernel(step, place_ref, heads_ref, turned_ref, right_ref, named_ref, tail_ref, kind_ref, rows_ref, *refs):
    state_ref, mine_ref, piece_refs, kid_ref = refs[0], refs[1], refs[2 : 2 + PIECES // 2], refs[2 + PIECES // 2]
    terms_out, carry_out, query_out, weight_out, main_ref, rest_ref = refs[3 + PIECES // 2 :]
    heads = heads_ref[...]
    width = heads.shape[0]
    square, core = place_ref[0], place_ref[1]
    half = PIECES // 2
    main, rest = cut(width)
    theirs = gather_pieces(piece_refs, kind_ref[...], width)
    for first, columns in ((core * half, mine_ref[...]), ((1 - core) * half, theirs)):
        for i in range(half):
            at = first + jnp.bitwise_xor(square, i)
            last = main * half + rest * i
            main_ref[at] = columns[main * i : main * (i + 1)]
            rest_ref[at, :rest] = columns[last : last + rest]
    grad = jnp.concatenate([main_ref[c] for c in range(PIECES)] + [rest_ref[c, :rest] for c in range(PIECES)], axis=0)
    state = state_ref[...] + jnp.sum(grad * grad, axis=0, keepdims=True) * (1.0 / width)
    rel_rows = rows_ref[...] - grad * (RATE / jnp.sqrt(state))
    query = heads * rel_rows
    weight = score(turned_ref[...], query, named_ref[...], tail_ref[...])
    grad_query = split_times(nn, right_ref[...], weight)
    put_terms(place_ref, grad_query * heads, kid_ref[step : step + 1], terms_out)
    carry_out[...] = grad_query * rel_rows
    query_out[...] = query
    weight_out[...] = weight


def relations_kernel(place_ref, rel_ref, relacc_ref, *refs):
    piece_refs, (rel_out, relacc_out, all_ref) = refs[:PIECES], refs[PIECES:]
    width = rel_ref.shape[0]
    order_pieces(place_ref, piece_refs, all_ref)
    accum, rate = next_accum(relacc_ref, all_ref, width)
    relacc_out[...] = accum[0] if len(relacc_out.shape) == 1 else accum
    blocks = rel_ref.shape[1] // LANES
    for j in range(blocks):
        lanes = slice(LANES * j, LANES * (j + 1))
        rel_out[:, lanes] = rel_ref[:, lanes] - take_rel_grad(all_ref, j, width, blocks) * rate[:, lanes]


def right_kernel(right_ref, query_ref, weight_ref, right_out):
    width = query_ref.shape[0]
    grad = times(nt, query_ref[...], weight_ref[...])
    put_packed(right_out, *adagrad(right_ref[:width], right_ref[width : width + 1], grad))


def update_kernel(
    step, left_ref, lacc_ref, carry_ref, hid_ref, right_ref, query_ref, weight_ref,
    left_out, lacc_out, right_out, racc_out,
):
    rows = left_ref.shape[1]
    grad = times_selector(nt, carry_ref[...], selector(hid_ref[step : step + 1], rows).astype(BF16))
    left_out[...], acc = adagrad(left_ref[...], lacc_ref[...], grad)
    lacc_out[...] = acc[0]
    width = left_ref.shape[0]
    grad = times(nt, query_ref[...], weight_ref[...])
    right_out[...], acc = adagrad(right_ref[:width], right_ref[width : width + 1], grad)
    racc_out[...] = acc[0]


HBM = pl.BlockSpec(memory_space=pltpu.HBM)
VMEM = pl.BlockSpec(memory_space=pltpu.VMEM)
SMEM = pl.BlockSpec(memory_space=pltpu.SMEM)
PARAMS = pltpu.CompilerParams(vmem_limit_bytes=40 * 1024 * 1024)


def call(kernel, outs, scratch=(), smem=0, hbm_outs=(), name=None, flops=0):
    def run(*given):
        moved = sum(math.prod(x.shape) for x in given) + sum(math.prod(getattr(shape, "shape", shape)) for shape in outs)
        in_specs = [SMEM if i < smem else VMEM for i in range(len(given))]
        return pl.pallas_call(
            kernel,
            out_shape=[jax.ShapeDtypeStruct(shape, F32) if isinstance(shape, tuple) else shape for shape in outs],
            in_specs=in_specs,
            out_specs=[HBM if i in hbm_outs else VMEM for i in range(len(outs))],
            scratch_shapes=list(scratch),
            compiler_params=PARAMS,
            cost_estimate=pl.CostEstimate(flops=flops, bytes_accessed=4 * moved, transcendentals=0),
            name=name,
        )(*given)

    return run


def swap(x, sizes, blk=0, shard=0, sub=0):
    n_blk, n_shard, n_sub = sizes

    def number(b, k, u):
        return (b * n_shard + k) * n_sub + u

    route = [
        (number(b, k, u), number(b ^ blk, k ^ shard, u ^ sub))
        for b in range(n_blk)
        for k in range(n_shard)
        for u in range(n_sub)
    ]
    return lax.ppermute(x, AXES, route)


def gray(i):
    return jnp.bitwise_and(jnp.bitwise_xor(i, i >> 1), 1)


def sum_pieces(terms, sizes, width, kinds, beside=None, work=lambda _: ()):
    half = PIECES // 2
    piece = (piece_rows(width, kinds), LANES)
    sent = terms[half:]
    if beside is not None:
        sent, beside = lax.optimization_barrier((sent, beside))
        beside = from_behind(beside, "blk")
    other = swap(sent, sizes, sub=1)
    got = [
        swap(jnp.concatenate([terms[i], other[i]], axis=0), sizes, blk=i & 1, shard=i >> 1) for i in range(1, half)
    ]
    if beside is not None:
        got[1], beside = lax.optimization_barrier((got[1], beside))
    total = call(functools.partial(chip_kernel, width, kinds), [piece], name="chip_terms")(terms, other)[0]
    for more in (got[1], got[2], got[0]):
        total = call(functools.partial(more_kernel, width, kinds), [piece], name="more_terms")(total, more)[0]
    reach = 4
    while reach <= sizes[0]:
        total = total + swap(total, sizes, blk=reach - 1)
        reach *= 2
    reach = 4
    while reach <= sizes[1]:
        total = total + swap(total, sizes, shard=reach - 1)
        reach *= 2
    total, aside = lax.optimization_barrier((total, work(beside)))
    mine = [total] + [swap(total, sizes, blk=i & 1, shard=i >> 1) for i in range(1, half)]
    return mine + [swap(x, sizes, sub=1) for x in mine], beside, aside


def from_behind(block, axis):
    n = lax.axis_size(axis)
    return lax.ppermute(block, axis, [((i - 1) % n, i) for i in range(n)])


def shards(
    head_table, head_accum, tail_table, tail_accum, relations, rel_accum, head_ids, tail_ids, rel_ids, neg_ids
):
    sizes = tuple(lax.axis_size(a) for a in AXES)
    steps = head_ids.shape[0]
    rows, width = head_table.shape
    kinds = relations.shape[0]
    core = lax.axis_index("sub")
    square = gray(lax.axis_index("shard")) * 2 + gray(lax.axis_index("blk"))
    place = jnp.stack([square, core]).astype(jnp.int32)

    left, lacc = head_table.T, head_accum[None]
    rel, relacc = relations.T, rel_accum[None]
    edges = head_ids.shape[1]
    table, state, each = (width, rows), (1, rows), (width, edges)
    cut_terms = (PIECES, term_rows(width, edges), LANES)
    given = (head_ids, tail_ids, rel_ids, neg_ids, left, tail_table.T, tail_accum[None], rel)
    right, terms, carry = pl.pallas_call(
        first_kernel,
        out_shape=[jax.ShapeDtypeStruct(shape, F32) for shape in [(width + 8, rows), cut_terms, each]],
        in_specs=[SMEM] + [HBM] * len(given),
        out_specs=[VMEM] * 3,
        scratch_shapes=[pltpu.VMEM(x.shape, x.dtype) for x in given] + [pltpu.SemaphoreType.DMA((len(given),))],
        compiler_params=PARAMS,
        name="first_step",
    )(place, *[pltpu.with_memory_space_constraint(x, pltpu.HBM) for x in given])
    all_pieces = pltpu.VMEM((PIECES, piece_rows(width, kinds), LANES), F32)
    half = PIECES // 2
    main, rest = cut(width)

    def short(*shape):
        return jax.ShapeDtypeStruct(shape, BF16)

    def relations(rel, relacc, summed, shape, name):
        return call(relations_kernel, [(width, kinds), shape], [all_pieces], smem=1, name=name)(
            place, rel, relacc, *summed
        )

    summed = None
    for step in range(1, steps):
        if step > 1:
            right = call(right_kernel, [(width + 8, rows)])(right, query, weight)[0]

        def ready(right, step=step, rel=rel, relacc=relacc, summed=summed):
            if summed is not None:
                rel, relacc = relations(rel, relacc, summed, (1, kinds), "relations")
            outs = [table, state, each, short(2 * rows, width), short(2 * width, rows), (rows, edges), (rows, edges)]
            outs += [short(kinds, edges), each, (1, edges)]
            return rel, relacc, *call(functools.partial(ready_kernel, step), outs, name="ready")(
                left, lacc, carry, right, rel, relacc, head_ids, tail_ids, rel_ids, neg_ids
            )

        summed, right, (rel, relacc, left, lacc, heads, turned, both, named, tail_sel, kind_sel, rel_rows, rel_state) = (
            sum_pieces(terms, sizes, width, kinds, right, ready)
        )
        mine = call(functools.partial(gather_kernel, width), [(half * (main + rest), edges)], name="gather")(
            *summed[:half], kind_sel
        )[0]
        terms, carry, query, weight = call(
            functools.partial(next_kernel, step),
            [cut_terms, each, each, (rows, edges)],
            [pltpu.VMEM((PIECES, main, edges), F32), pltpu.VMEM((PIECES, 8, edges), F32)],
            smem=1,
            name="next_step",
        )(place, heads, turned, both, named, tail_sel, kind_sel, rel_rows, rel_state, mine, *summed[half:], rel_ids)

    def update(_):
        return *relations(rel, relacc, summed, (1, kinds), "relations"), *call(
            functools.partial(update_kernel, steps - 1), [table, (rows,), table, (rows,)], name="last_update"
        )(left, lacc, carry, head_ids, right, query, weight)

    last, _, (rel, relacc, left, lacc, right, racc) = sum_pieces(terms, sizes, width, kinds, work=update)
    rel, relacc = relations(rel, relacc, last, (kinds,), "last_relations")
    return (left.T, lacc, right.T, racc, rel.T, relacc)


def solution(mesh):
    every = ("groups", "blk", "shard", "sub")
    return jax.shard_map(
        shards,
        mesh=mesh,
        in_specs=(
            P(every, None),
            P(every),
            P(every, None),
            P(every),
            P("groups", None),
            P("groups"),
            P(None, every),
            P(None, every),
            P(None, every),
            P(None, every, None),
        ),
        out_specs=(P(every, None), P(every), P(every, None), P(every), P("groups", None), P("groups")),
        check_vma=False,
    )
```

```python
import functools
import math

import jax
import jax.numpy as jnp
from jax import lax
from jax.experimental import pallas as pl
from jax.experimental.pallas import tpu as pltpu
from jax.sharding import PartitionSpec as P

RATE = 0.1
AXES = ("blk", "shard", "sub")
LANES = 128
PIECES = 8
F32 = jnp.float32
BF16 = jnp.bfloat16


def halves(x):
    high = x.astype(BF16)
    return high, (x - high.astype(F32)).astype(BF16)


def nn(a, b):
    return lax.dot_general(a, b, (((1,), (0,)), ((), ())), preferred_element_type=F32)


def nt(a, b):
    return lax.dot_general(a, b, (((1,), (1,)), ((), ())), preferred_element_type=F32)


def stack(x):
    high = x.astype(BF16).astype(F32)
    return jnp.concatenate([high, x - high], axis=0).astype(BF16)


def times_selector(dot, x, selector):
    rows = x.shape[0]
    both = dot(stack(x), selector)
    return both[:rows] + both[rows:]


def times(dot, a, b):
    a_high, a_low = halves(a)
    b_high, b_low = halves(b)
    rows = a.shape[0]
    both = dot(jnp.concatenate([a_high, a_low], axis=0), b_high)
    return both[:rows] + (both[rows:] + dot(a_high, b_low))


def selector(ids, rows):
    return (lax.broadcasted_iota(jnp.int32, (rows, ids.shape[1]), 0) == ids).astype(F32)


def adagrad(weights, accum, grads):
    accum = accum + jnp.sum(grads * grads, axis=0, keepdims=True) * (1.0 / grads.shape[0])
    return weights - grads * (RATE / jnp.sqrt(accum)), accum


def prepare(right, tail_ids, negative):
    rows = right.shape[1]
    count, negs = negative.shape
    named = []
    for c in range(count):
        hits = lax.broadcasted_iota(jnp.int32, (rows, negs), 0) == negative[c : c + 1]
        share = jnp.sum(hits.astype(F32), axis=1, keepdims=True) * (1.0 / negs)
        named.append(jnp.broadcast_to(share, (rows, tail_ids.shape[1] // count)))
    return jnp.concatenate(named, axis=1), selector(tail_ids, rows)


def split_times(dot, a_both, b):
    rows = a_both.shape[0] // 2
    b_high, b_low = halves(b)
    both = dot(a_both, b_high)
    return both[:rows] + (both[rows:] + dot(a_both[:rows], b_low))


def score(right_turned, query, named, tail_sel):
    scores = split_times(nn, right_turned, query)
    tiny = jnp.exp(-jnp.abs(scores))
    inverse = 1.0 / (1.0 + tiny)
    up = scores >= 0
    sig = jnp.where(up, 1.0, tiny) * inverse
    sig_minus = jnp.where(up, tiny, 1.0) * inverse
    return named * sig - tail_sel * sig_minus


def cut(width):
    main = width // (8 * PIECES) * 8
    return main, width // PIECES - main


def piece_rows(width, kinds):
    return -(-(width // PIECES) * kinds // LANES // 8) * 8


def term_rows(width, edges):
    return edges // LANES * cut(width)[0] + 8


def put_terms(place_ref, terms, kinds, out_ref):
    square, core = place_ref[0], place_ref[1]
    width, edges = terms.shape
    half = PIECES // 2
    main, rest = cut(width)
    tiles = [slice(LANES * j, LANES * (j + 1)) for j in range(edges // LANES)]
    ids = [kinds[:, lanes].astype(F32) for lanes in tiles]
    ids.append(jnp.zeros((8 - len(tiles) * (rest + 1), LANES), F32))
    for c in range(PIECES):
        at = jnp.bitwise_xor(c // half, core) * half + jnp.bitwise_xor(c % half, square)
        last = main * PIECES + rest * c
        for j, lanes in enumerate(tiles):
            out_ref[at, main * j : main * (j + 1)] = terms[main * c : main * (c + 1), lanes]
        out_ref[at, main * len(tiles) :] = jnp.concatenate(
            [terms[last : last + rest, lanes] for lanes in tiles] + ids, axis=0
        )


def turn(x, by):
    return [x[by:], x[:by]] if by else [x]


def sum_terms(width, kinds, parts):
    main, rest = cut(width)
    total = None
    for part in parts:
        tiles = part.shape[0] // main
        below = part[main * tiles :]
        each = [
            jnp.concatenate([part[main * j : main * (j + 1)]] + turn(below, rest * j), axis=0)
            for j in range(tiles)
        ]
        first = rest * tiles
        ids = jnp.concatenate([below[first + j : first + j + 1] for j in range(tiles)], axis=1)
        both = stack(jnp.concatenate(each, axis=1))
        grad = nt(both, selector(ids.astype(jnp.int32), kinds).astype(BF16))
        grad = grad[: main + 8] + grad[main + 8 :]
        total = grad if total is None else total + grad
    return total


def put_piece(grad, width, out_ref, before_ref=None):
    main, rest = cut(width)
    blocks = grad.shape[1] // LANES
    for j in range(blocks):
        lanes = slice(LANES * j, LANES * (j + 1))
        for rows, part in (
            (slice(main * j, main * (j + 1)), grad[:main, lanes]),
            (slice(main * blocks + rest * j, main * blocks + rest * (j + 1)), grad[main : main + rest, lanes]),
        ):
            out_ref[rows] = part if before_ref is None else before_ref[rows] + part
    end = (main + rest) * blocks
    out_ref[end:] = jnp.zeros((out_ref.shape[0] - end, LANES), F32)


def chip_kernel(width, kinds, own_ref, other_ref, out_ref):
    put_piece(sum_terms(width, kinds, [own_ref[0], other_ref[0]]), width, out_ref)


def more_kernel(width, kinds, total_ref, terms_ref, out_ref):
    rows = terms_ref.shape[0] // 2
    put_piece(sum_terms(width, kinds, [terms_ref[:rows], terms_ref[rows:]]), width, out_ref, total_ref)


def order_pieces(place_ref, piece_refs, all_ref):
    square, core = place_ref[0], place_ref[1]
    half = PIECES // 2
    for i in range(half):
        piece = jnp.bitwise_xor(square, i)
        all_ref[core * half + piece] = piece_refs[i][...]
        all_ref[(1 - core) * half + piece] = piece_refs[half + i][...]


def take_rel_grad(all_ref, j, width, blocks):
    main, rest = cut(width)
    first, last = main * j, main * blocks + rest * j
    return jnp.concatenate(
        [all_ref[c, first : first + main] for c in range(PIECES)]
        + [all_ref[c, last : last + rest] for c in range(PIECES)],
        axis=0,
    )


def next_accum(relacc_ref, all_ref, width):
    squares = []
    blocks = relacc_ref.shape[1] // LANES
    for j in range(blocks):
        grad = take_rel_grad(all_ref, j, width, blocks)
        squares.append(jnp.sum(grad * grad, axis=0, keepdims=True))
    accum = relacc_ref[...] + jnp.concatenate(squares, axis=1) * (1.0 / width)
    return accum, RATE / jnp.sqrt(accum)


def put_packed(out_ref, right, acc):
    width = right.shape[0]
    out_ref[:width] = right
    out_ref[width:] = jnp.broadcast_to(acc, (8, acc.shape[1]))


def first_kernel(place_ref, *refs):
    given, (right_out, terms_out, carry_out), held, sems = refs[:8], refs[8:11], refs[11:19], refs[19]
    copies = [pltpu.make_async_copy(a, b, sems.at[i]) for i, (a, b) in enumerate(zip(given, held))]
    for copy in copies:
        copy.start()
    hid_ref, tid_ref, kid_ref, nid_ref, left_ref, right_ref, racc_ref, rel_ref = held
    for copy in copies[:5]:
        copy.wait()
    head_sel = selector(hid_ref[0:1], left_ref.shape[1]).astype(BF16)
    kind_sel = selector(kid_ref[0:1], rel_ref.shape[1]).astype(BF16)
    heads = times_selector(nn, left_ref[...], head_sel)
    for copy in copies[5:]:
        copy.wait()
    right = right_ref[...]
    rel_rows = times_selector(nn, rel_ref[...], kind_sel)
    query = heads * rel_rows
    weight = score(stack(right.T), query, *prepare(right, tid_ref[0:1], nid_ref[0]))
    grad_query = times(nn, right, weight)
    put_terms(place_ref, grad_query * heads, kid_ref[0:1], terms_out)
    put_packed(right_out, *adagrad(right, racc_ref[...], times(nt, query, weight)))
    carry_out[...] = grad_query * rel_rows


def ready_kernel(
    step, left_ref, lacc_ref, carry_ref, right_ref, rel_ref, relacc_ref, hid_ref, tid_ref, kid_ref, nid_ref,
    left_out, lacc_out, heads_out, turned_out, right_out, named_out, tail_out, kind_out, rows_out, state_out,
):
    width, rows = left_ref.shape
    grad = times_selector(nt, carry_ref[...], selector(hid_ref[step - 1 : step], rows).astype(BF16))
    left, lacc_out[...] = adagrad(left_ref[...], lacc_ref[...], grad)
    left_out[...] = left
    heads_out[...] = times_selector(nn, left, selector(hid_ref[step : step + 1], rows).astype(BF16))
    right = right_ref[:width]
    turned_out[...] = stack(right.T)
    right_out[...] = stack(right)
    named_out[...], tail_out[...] = prepare(right, tid_ref[step : step + 1], nid_ref[step])
    kind_sel = selector(kid_ref[step : step + 1], rel_ref.shape[1]).astype(BF16)
    kind_out[...] = kind_sel
    state = jnp.broadcast_to(relacc_ref[...], (8, rel_ref.shape[1]))
    rel_rows = times_selector(nn, jnp.concatenate([rel_ref[...], state], axis=0), kind_sel)
    rows_out[...] = rel_rows[:width]
    state_out[...] = rel_rows[width : width + 1]


def gather_pieces(piece_refs, kind_sel, width):
    main, rest = cut(width)
    blocks = kind_sel.shape[0] // LANES
    mains = [jnp.concatenate([ref[main * j : main * (j + 1)] for j in range(blocks)], axis=1) for ref in piece_refs]
    first = main * blocks
    rests = [
        jnp.concatenate([ref[first + rest * j : first + rest * (j + 1)] for j in range(blocks)], axis=1)
        for ref in piece_refs
    ]
    return times_selector(nn, jnp.concatenate(mains + rests, axis=0), kind_sel)


def gather_kernel(width, *refs):
    refs[-1][...] = gather_pieces(refs[:-2], refs[-2][...], width)


def next_kernel(step, place_ref, heads_ref, turned_ref, right_ref, named_ref, tail_ref, kind_ref, rows_ref, *refs):
    state_ref, mine_ref, piece_refs, kid_ref = refs[0], refs[1], refs[2 : 2 + PIECES // 2], refs[2 + PIECES // 2]
    terms_out, carry_out, query_out, weight_out, main_ref, rest_ref = refs[3 + PIECES // 2 :]
    heads = heads_ref[...]
    width = heads.shape[0]
    square, core = place_ref[0], place_ref[1]
    half = PIECES // 2
    main, rest = cut(width)
    theirs = gather_pieces(piece_refs, kind_ref[...], width)
    for first, columns in ((core * half, mine_ref[...]), ((1 - core) * half, theirs)):
        for i in range(half):
            at = first + jnp.bitwise_xor(square, i)
            last = main * half + rest * i
            main_ref[at] = columns[main * i : main * (i + 1)]
            rest_ref[at, :rest] = columns[last : last + rest]
    grad = jnp.concatenate([main_ref[c] for c in range(PIECES)] + [rest_ref[c, :rest] for c in range(PIECES)], axis=0)
    state = state_ref[...] + jnp.sum(grad * grad, axis=0, keepdims=True) * (1.0 / width)
    rel_rows = rows_ref[...] - grad * (RATE / jnp.sqrt(state))
    query = heads * rel_rows
    weight = score(turned_ref[...], query, named_ref[...], tail_ref[...])
    grad_query = split_times(nn, right_ref[...], weight)
    put_terms(place_ref, grad_query * heads, kid_ref[step : step + 1], terms_out)
    carry_out[...] = grad_query * rel_rows
    query_out[...] = query
    weight_out[...] = weight


def relations_kernel(place_ref, rel_ref, relacc_ref, *refs):
    piece_refs, (rel_out, relacc_out, all_ref) = refs[:PIECES], refs[PIECES:]
    width = rel_ref.shape[0]
    order_pieces(place_ref, piece_refs, all_ref)
    accum, rate = next_accum(relacc_ref, all_ref, width)
    relacc_out[...] = accum[0] if len(relacc_out.shape) == 1 else accum
    blocks = rel_ref.shape[1] // LANES
    for j in range(blocks):
        lanes = slice(LANES * j, LANES * (j + 1))
        rel_out[:, lanes] = rel_ref[:, lanes] - take_rel_grad(all_ref, j, width, blocks) * rate[:, lanes]


def right_kernel(right_ref, query_ref, weight_ref, right_out):
    width = query_ref.shape[0]
    grad = times(nt, query_ref[...], weight_ref[...])
    put_packed(right_out, *adagrad(right_ref[:width], right_ref[width : width + 1], grad))


def update_kernel(
    step, left_ref, lacc_ref, carry_ref, hid_ref, right_ref, query_ref, weight_ref,
    left_out, lacc_out, right_out, racc_out,
):
    rows = left_ref.shape[1]
    grad = times_selector(nt, carry_ref[...], selector(hid_ref[step : step + 1], rows).astype(BF16))
    left_out[...], acc = adagrad(left_ref[...], lacc_ref[...], grad)
    lacc_out[...] = acc[0]
    width = left_ref.shape[0]
    grad = times(nt, query_ref[...], weight_ref[...])
    right_out[...], acc = adagrad(right_ref[:width], right_ref[width : width + 1], grad)
    racc_out[...] = acc[0]


HBM = pl.BlockSpec(memory_space=pltpu.HBM)
VMEM = pl.BlockSpec(memory_space=pltpu.VMEM)
SMEM = pl.BlockSpec(memory_space=pltpu.SMEM)
PARAMS = pltpu.CompilerParams(vmem_limit_bytes=40 * 1024 * 1024)


def call(kernel, outs, scratch=(), smem=0, hbm_outs=(), name=None, flops=0):
    def run(*given):
        moved = sum(math.prod(x.shape) for x in given) + sum(math.prod(getattr(shape, "shape", shape)) for shape in outs)
        in_specs = [SMEM if i < smem else VMEM for i in range(len(given))]
        return pl.pallas_call(
            kernel,
            out_shape=[jax.ShapeDtypeStruct(shape, F32) if isinstance(shape, tuple) else shape for shape in outs],
            in_specs=in_specs,
            out_specs=[HBM if i in hbm_outs else VMEM for i in range(len(outs))],
            scratch_shapes=list(scratch),
            compiler_params=PARAMS,
            cost_estimate=pl.CostEstimate(flops=flops, bytes_accessed=4 * moved, transcendentals=0),
            name=name,
        )(*given)

    return run


def swap(x, sizes, blk=0, shard=0, sub=0):
    n_blk, n_shard, n_sub = sizes

    def number(b, k, u):
        return (b * n_shard + k) * n_sub + u

    route = [
        (number(b, k, u), number(b ^ blk, k ^ shard, u ^ sub))
        for b in range(n_blk)
        for k in range(n_shard)
        for u in range(n_sub)
    ]
    return lax.ppermute(x, AXES, route)


def gray(i):
    return jnp.bitwise_and(jnp.bitwise_xor(i, i >> 1), 1)


def sum_pieces(terms, sizes, width, kinds, beside=None, work=lambda _: ()):
    half = PIECES // 2
    piece = (piece_rows(width, kinds), LANES)
    sent = terms[half:]
    if beside is not None:
        sent, beside = lax.optimization_barrier((sent, beside))
        beside = from_behind(beside, "blk")
    other = swap(sent, sizes, sub=1)
    got = [
        swap(jnp.concatenate([terms[i], other[i]], axis=0), sizes, blk=i & 1, shard=i >> 1) for i in range(1, half)
    ]
    if beside is not None:
        got[1], beside = lax.optimization_barrier((got[1], beside))
    total = call(functools.partial(chip_kernel, width, kinds), [piece], name="chip_terms")(terms, other)[0]
    for more in (got[1], got[2], got[0]):
        total = call(functools.partial(more_kernel, width, kinds), [piece], name="more_terms")(total, more)[0]
    reach = 4
    while reach <= sizes[0]:
        total = total + swap(total, sizes, blk=reach - 1)
        reach *= 2
    reach = 4
    while reach <= sizes[1]:
        total = total + swap(total, sizes, shard=reach - 1)
        reach *= 2
    total, aside = lax.optimization_barrier((total, work(beside)))
    mine = [total] + [swap(total, sizes, blk=i & 1, shard=i >> 1) for i in range(1, half)]
    return mine + [swap(x, sizes, sub=1) for x in mine], beside, aside


def from_behind(block, axis):
    n = lax.axis_size(axis)
    return lax.ppermute(block, axis, [((i - 1) % n, i) for i in range(n)])


def shards(
    head_table, head_accum, tail_table, tail_accum, relations, rel_accum, head_ids, tail_ids, rel_ids, neg_ids
):
    sizes = tuple(lax.axis_size(a) for a in AXES)
    steps = head_ids.shape[0]
    rows, width = head_table.shape
    kinds = relations.shape[0]
    core = lax.axis_index("sub")
    square = gray(lax.axis_index("shard")) * 2 + gray(lax.axis_index("blk"))
    place = jnp.stack([square, core]).astype(jnp.int32)

    left, lacc = head_table.T, head_accum[None]
    rel, relacc = relations.T, rel_accum[None]
    edges = head_ids.shape[1]
    table, state, each = (width, rows), (1, rows), (width, edges)
    cut_terms = (PIECES, term_rows(width, edges), LANES)
    given = (head_ids, tail_ids, rel_ids, neg_ids, left, tail_table.T, tail_accum[None], rel)
    right, terms, carry = pl.pallas_call(
        first_kernel,
        out_shape=[jax.ShapeDtypeStruct(shape, F32) for shape in [(width + 8, rows), cut_terms, each]],
        in_specs=[SMEM] + [HBM] * len(given),
        out_specs=[VMEM] * 3,
        scratch_shapes=[pltpu.VMEM(x.shape, x.dtype) for x in given] + [pltpu.SemaphoreType.DMA((len(given),))],
        compiler_params=PARAMS,
        name="first_step",
    )(place, *[pltpu.with_memory_space_constraint(x, pltpu.HBM) for x in given])
    all_pieces = pltpu.VMEM((PIECES, piece_rows(width, kinds), LANES), F32)
    half = PIECES // 2
    main, rest = cut(width)

    def short(*shape):
        return jax.ShapeDtypeStruct(shape, BF16)

    def relations(rel, relacc, summed, shape, name):
        return call(relations_kernel, [(width, kinds), shape], [all_pieces], smem=1, name=name)(
            place, rel, relacc, *summed
        )

    summed = None
    for step in range(1, steps):
        if step > 1:
            right = call(right_kernel, [(width + 8, rows)])(right, query, weight)[0]

        def ready(right, step=step, rel=rel, relacc=relacc, summed=summed):
            if summed is not None:
                rel, relacc = relations(rel, relacc, summed, (1, kinds), "relations")
            outs = [table, state, each, short(2 * rows, width), short(2 * width, rows), (rows, edges), (rows, edges)]
            outs += [short(kinds, edges), each, (1, edges)]
            return rel, relacc, *call(functools.partial(ready_kernel, step), outs, name="ready")(
                left, lacc, carry, right, rel, relacc, head_ids, tail_ids, rel_ids, neg_ids
            )

        summed, right, (rel, relacc, left, lacc, heads, turned, both, named, tail_sel, kind_sel, rel_rows, rel_state) = (
            sum_pieces(terms, sizes, width, kinds, right, ready)
        )
        mine = call(functools.partial(gather_kernel, width), [(half * (main + rest), edges)], name="gather")(
            *summed[:half], kind_sel
        )[0]
        terms, carry, query, weight = call(
            functools.partial(next_kernel, step),
            [cut_terms, each, each, (rows, edges)],
            [pltpu.VMEM((PIECES, main, edges), F32), pltpu.VMEM((PIECES, 8, edges), F32)],
            smem=1,
            name="next_step",
        )(place, heads, turned, both, named, tail_sel, kind_sel, rel_rows, rel_state, mine, *summed[half:], rel_ids)

    def update(_):
        return *relations(rel, relacc, summed, (1, kinds), "relations"), *call(
            functools.partial(update_kernel, steps - 1), [table, (rows,), table, (rows,)], name="last_update"
        )(left, lacc, carry, head_ids, right, query, weight)

    last, _, (rel, relacc, left, lacc, right, racc) = sum_pieces(terms, sizes, width, kinds, work=update)
    rel, relacc = relations(rel, relacc, last, (kinds,), "last_relations")
    return (left.T, lacc, right.T, racc, rel.T, relacc)


def solution(mesh):
    every = ("groups", "blk", "shard", "sub")
    return jax.shard_map(
        shards,
        mesh=mesh,
        in_specs=(
            P(every, None),
            P(every),
            P(every, None),
            P(every),
            P("groups", None),
            P("groups"),
            P(None, every),
            P(None, every),
            P(None, every),
            P(None, every, None),
        ),
        out_specs=(P(every, None), P(every), P(every, None), P(every), P("groups", None), P("groups")),
        check_vma=False,
    )
```

```python
import functools
import math

import jax
import jax.numpy as jnp
from jax import lax
from jax.experimental import pallas as pl
from jax.experimental.pallas import tpu as pltpu
from jax.sharding import PartitionSpec as P

RATE = 0.1
AXES = ("blk", "shard", "sub")
LANES = 128
PIECES = 8
F32 = jnp.float32
BF16 = jnp.bfloat16


def halves(x):
    high = x.astype(BF16)
    return high, (x - high.astype(F32)).astype(BF16)


def nn(a, b):
    return lax.dot_general(a, b, (((1,), (0,)), ((), ())), preferred_element_type=F32)


def nt(a, b):
    return lax.dot_general(a, b, (((1,), (1,)), ((), ())), preferred_element_type=F32)


def stack(x):
    high = x.astype(BF16).astype(F32)
    return jnp.concatenate([high, x - high], axis=0).astype(BF16)


def times_selector(dot, x, selector):
    rows = x.shape[0]
    both = dot(stack(x), selector)
    return both[:rows] + both[rows:]


def times(dot, a, b):
    a_high, a_low = halves(a)
    b_high, b_low = halves(b)
    rows = a.shape[0]
    both = dot(jnp.concatenate([a_high, a_low], axis=0), b_high)
    return both[:rows] + (both[rows:] + dot(a_high, b_low))


def selector(ids, rows):
    return (lax.broadcasted_iota(jnp.int32, (rows, ids.shape[1]), 0) == ids).astype(F32)


def adagrad(weights, accum, grads):
    accum = accum + jnp.sum(grads * grads, axis=0, keepdims=True) * (1.0 / grads.shape[0])
    return weights - grads * (RATE / jnp.sqrt(accum)), accum


def prepare(right, tail_ids, negative):
    rows = right.shape[1]
    count, negs = negative.shape
    named = []
    for c in range(count):
        hits = lax.broadcasted_iota(jnp.int32, (rows, negs), 0) == negative[c : c + 1]
        share = jnp.sum(hits.astype(F32), axis=1, keepdims=True) * (1.0 / negs)
        named.append(jnp.broadcast_to(share, (rows, tail_ids.shape[1] // count)))
    return jnp.concatenate(named, axis=1), selector(tail_ids, rows)


def split_times(dot, a_both, b):
    rows = a_both.shape[0] // 2
    b_high, b_low = halves(b)
    both = dot(a_both, b_high)
    return both[:rows] + (both[rows:] + dot(a_both[:rows], b_low))


def score(right_turned, query, named, tail_sel):
    scores = split_times(nn, right_turned, query)
    tiny = jnp.exp(-jnp.abs(scores))
    inverse = 1.0 / (1.0 + tiny)
    up = scores >= 0
    sig = jnp.where(up, 1.0, tiny) * inverse
    sig_minus = jnp.where(up, tiny, 1.0) * inverse
    return named * sig - tail_sel * sig_minus


def gray(i):
    return jnp.bitwise_and(jnp.bitwise_xor(i, i >> 1), 1)


def place():
    return gray(lax.axis_index("shard")) * 2 + gray(lax.axis_index("blk")), lax.axis_index("sub")


def cut(width):
    main = width // (8 * PIECES) * 8
    return main, width // PIECES - main


def piece_rows(width, kinds):
    return -(-(width // PIECES) * kinds // LANES // 8) * 8


def term_rows(width, edges):
    return edges // LANES * cut(width)[0] + 8


def put_terms(terms, kinds, out_ref):
    square, core = place()
    width, edges = terms.shape
    half = PIECES // 2
    main, rest = cut(width)
    tiles = [slice(LANES * j, LANES * (j + 1)) for j in range(edges // LANES)]
    ids = [kinds[:, lanes].astype(F32) for lanes in tiles]
    ids.append(jnp.zeros((8 - len(tiles) * (rest + 1), LANES), F32))
    for c in range(PIECES):
        at = jnp.bitwise_xor(c // half, core) * half + jnp.bitwise_xor(c % half, square)
        last = main * PIECES + rest * c
        for j, lanes in enumerate(tiles):
            out_ref[at, main * j : main * (j + 1)] = terms[main * c : main * (c + 1), lanes]
        out_ref[at, main * len(tiles) :] = jnp.concatenate(
            [terms[last : last + rest, lanes] for lanes in tiles] + ids, axis=0
        )


def turn(x, by):
    return [x[by:], x[:by]] if by else [x]


def sum_terms(width, kinds, parts):
    main, rest = cut(width)
    total = None
    for part in parts:
        tiles = part.shape[0] // main
        below = part[main * tiles :]
        each = [
            jnp.concatenate([part[main * j : main * (j + 1)]] + turn(below, rest * j), axis=0)
            for j in range(tiles)
        ]
        first = rest * tiles
        ids = jnp.concatenate([below[first + j : first + j + 1] for j in range(tiles)], axis=1)
        both = stack(jnp.concatenate(each, axis=1))
        grad = nt(both, selector(ids.astype(jnp.int32), kinds).astype(BF16))
        grad = grad[: main + 8] + grad[main + 8 :]
        total = grad if total is None else total + grad
    return total


def put_piece(grad, width, out_ref, before_ref=None):
    main, rest = cut(width)
    blocks = grad.shape[1] // LANES
    for j in range(blocks):
        lanes = slice(LANES * j, LANES * (j + 1))
        for rows, part in (
            (slice(main * j, main * (j + 1)), grad[:main, lanes]),
            (slice(main * blocks + rest * j, main * blocks + rest * (j + 1)), grad[main : main + rest, lanes]),
        ):
            out_ref[rows] = part if before_ref is None else before_ref[rows] + part
    end = (main + rest) * blocks
    out_ref[end:] = jnp.zeros((out_ref.shape[0] - end, LANES), F32)


def chip_kernel(width, kinds, own_ref, other_ref, out_ref):
    put_piece(sum_terms(width, kinds, [own_ref[0], other_ref[0]]), width, out_ref)


def more_kernel(width, kinds, total_ref, terms_ref, out_ref):
    rows = terms_ref.shape[0] // 2
    put_piece(sum_terms(width, kinds, [terms_ref[:rows], terms_ref[rows:]]), width, out_ref, total_ref)


def order_pieces(piece_refs, all_ref):
    square, core = place()
    half = PIECES // 2
    for i in range(half):
        piece = jnp.bitwise_xor(square, i)
        all_ref[core * half + piece] = piece_refs[i][...]
        all_ref[(1 - core) * half + piece] = piece_refs[half + i][...]


def take_rel_grad(all_ref, j, width, blocks):
    main, rest = cut(width)
    first, last = main * j, main * blocks + rest * j
    return jnp.concatenate(
        [all_ref[c, first : first + main] for c in range(PIECES)]
        + [all_ref[c, last : last + rest] for c in range(PIECES)],
        axis=0,
    )


def next_accum(relacc_ref, all_ref, width):
    squares = []
    blocks = relacc_ref.shape[1] // LANES
    for j in range(blocks):
        grad = take_rel_grad(all_ref, j, width, blocks)
        squares.append(jnp.sum(grad * grad, axis=0, keepdims=True))
    accum = relacc_ref[...] + jnp.concatenate(squares, axis=1) * (1.0 / width)
    return accum, RATE / jnp.sqrt(accum)


def put_packed(out_ref, right, acc):
    width = right.shape[0]
    out_ref[:width] = right
    out_ref[width:] = jnp.broadcast_to(acc, (8, acc.shape[1]))


def first_kernel(*refs):
    given, (right_out, terms_out, carry_out), held, sems = refs[:8], refs[8:11], refs[11:19], refs[19]
    copies = [pltpu.make_async_copy(a, b, sems.at[i]) for i, (a, b) in enumerate(zip(given, held))]
    for copy in copies:
        copy.start()
    hid_ref, tid_ref, kid_ref, nid_ref, left_ref, right_ref, racc_ref, rel_ref = held
    for copy in copies[:5]:
        copy.wait()
    head_sel = selector(hid_ref[0:1], left_ref.shape[1]).astype(BF16)
    kind_sel = selector(kid_ref[0:1], rel_ref.shape[1]).astype(BF16)
    heads = times_selector(nn, left_ref[...], head_sel)
    for copy in copies[5:]:
        copy.wait()
    right = right_ref[...]
    rel_rows = times_selector(nn, rel_ref[...], kind_sel)
    query = heads * rel_rows
    weight = score(stack(right.T), query, *prepare(right, tid_ref[0:1], nid_ref[0]))
    grad_query = times(nn, right, weight)
    put_terms(grad_query * heads, kid_ref[0:1], terms_out)
    put_packed(right_out, *adagrad(right, racc_ref[...], times(nt, query, weight)))
    carry_out[...] = grad_query * rel_rows


def ready_kernel(
    step, left_ref, lacc_ref, carry_ref, right_ref, rel_ref, relacc_ref, hid_ref, tid_ref, kid_ref, nid_ref,
    left_out, lacc_out, heads_out, turned_out, right_out, named_out, tail_out, kind_out, rows_out, state_out,
):
    width, rows = left_ref.shape
    grad = times_selector(nt, carry_ref[...], selector(hid_ref[step - 1 : step], rows).astype(BF16))
    left, lacc_out[...] = adagrad(left_ref[...], lacc_ref[...], grad)
    left_out[...] = left
    heads_out[...] = times_selector(nn, left, selector(hid_ref[step : step + 1], rows).astype(BF16))
    right = right_ref[:width]
    turned_out[...] = stack(right.T)
    right_out[...] = stack(right)
    named_out[...], tail_out[...] = prepare(right, tid_ref[step : step + 1], nid_ref[step])
    kind_sel = selector(kid_ref[step : step + 1], rel_ref.shape[1]).astype(BF16)
    kind_out[...] = kind_sel
    state = jnp.broadcast_to(relacc_ref[...], (8, rel_ref.shape[1]))
    rel_rows = times_selector(nn, jnp.concatenate([rel_ref[...], state], axis=0), kind_sel)
    rows_out[...] = rel_rows[:width]
    state_out[...] = rel_rows[width : width + 1]


def gather_pieces(piece_refs, kind_sel, width):
    main, rest = cut(width)
    blocks = kind_sel.shape[0] // LANES
    mains = [jnp.concatenate([ref[main * j : main * (j + 1)] for j in range(blocks)], axis=1) for ref in piece_refs]
    first = main * blocks
    rests = [
        jnp.concatenate([ref[first + rest * j : first + rest * (j + 1)] for j in range(blocks)], axis=1)
        for ref in piece_refs
    ]
    return times_selector(nn, jnp.concatenate(mains + rests, axis=0), kind_sel)


def gather_kernel(width, *refs):
    refs[-1][...] = gather_pieces(refs[:-2], refs[-2][...], width)


def next_kernel(step, heads_ref, turned_ref, right_ref, named_ref, tail_ref, kind_ref, rows_ref, *refs):
    state_ref, mine_ref, piece_refs, kid_ref = refs[0], refs[1], refs[2 : 2 + PIECES // 2], refs[2 + PIECES // 2]
    terms_out, carry_out, query_out, weight_out, main_ref, rest_ref = refs[3 + PIECES // 2 :]
    heads = heads_ref[...]
    width = heads.shape[0]
    square, core = place()
    half = PIECES // 2
    main, rest = cut(width)
    theirs = gather_pieces(piece_refs, kind_ref[...], width)
    for first, columns in ((core * half, mine_ref[...]), ((1 - core) * half, theirs)):
        for i in range(half):
            at = first + jnp.bitwise_xor(square, i)
            last = main * half + rest * i
            main_ref[at] = columns[main * i : main * (i + 1)]
            rest_ref[at, :rest] = columns[last : last + rest]
    grad = jnp.concatenate([main_ref[c] for c in range(PIECES)] + [rest_ref[c, :rest] for c in range(PIECES)], axis=0)
    state = state_ref[...] + jnp.sum(grad * grad, axis=0, keepdims=True) * (1.0 / width)
    rel_rows = rows_ref[...] - grad * (RATE / jnp.sqrt(state))
    query = heads * rel_rows
    weight = score(turned_ref[...], query, named_ref[...], tail_ref[...])
    grad_query = split_times(nn, right_ref[...], weight)
    put_terms(grad_query * heads, kid_ref[step : step + 1], terms_out)
    carry_out[...] = grad_query * rel_rows
    query_out[...] = query
    weight_out[...] = weight


def relations_kernel(rel_ref, relacc_ref, *refs):
    piece_refs, (rel_out, relacc_out, all_ref) = refs[:PIECES], refs[PIECES:]
    width = rel_ref.shape[0]
    order_pieces(piece_refs, all_ref)
    accum, rate = next_accum(relacc_ref, all_ref, width)
    relacc_out[...] = accum[0] if len(relacc_out.shape) == 1 else accum
    blocks = rel_ref.shape[1] // LANES
    for j in range(blocks):
        lanes = slice(LANES * j, LANES * (j + 1))
        rel_out[:, lanes] = rel_ref[:, lanes] - take_rel_grad(all_ref, j, width, blocks) * rate[:, lanes]


def right_kernel(right_ref, query_ref, weight_ref, right_out):
    width = query_ref.shape[0]
    grad = times(nt, query_ref[...], weight_ref[...])
    put_packed(right_out, *adagrad(right_ref[:width], right_ref[width : width + 1], grad))


def update_kernel(
    step, left_ref, lacc_ref, carry_ref, hid_ref, right_ref, query_ref, weight_ref,
    left_out, lacc_out, right_out, racc_out,
):
    rows = left_ref.shape[1]
    grad = times_selector(nt, carry_ref[...], selector(hid_ref[step : step + 1], rows).astype(BF16))
    left_out[...], acc = adagrad(left_ref[...], lacc_ref[...], grad)
    lacc_out[...] = acc[0]
    width = left_ref.shape[0]
    grad = times(nt, query_ref[...], weight_ref[...])
    right_out[...], acc = adagrad(right_ref[:width], right_ref[width : width + 1], grad)
    racc_out[...] = acc[0]


HBM = pl.BlockSpec(memory_space=pltpu.HBM)
VMEM = pl.BlockSpec(memory_space=pltpu.VMEM)
PARAMS = pltpu.CompilerParams(vmem_limit_bytes=40 * 1024 * 1024)


def call(kernel, outs, scratch=(), hbm_outs=(), name=None, flops=0):
    def run(*given):
        moved = sum(math.prod(x.shape) for x in given) + sum(math.prod(getattr(shape, "shape", shape)) for shape in outs)
        return pl.pallas_call(
            kernel,
            out_shape=[jax.ShapeDtypeStruct(shape, F32) if isinstance(shape, tuple) else shape for shape in outs],
            in_specs=[VMEM] * len(given),
            out_specs=[HBM if i in hbm_outs else VMEM for i in range(len(outs))],
            scratch_shapes=list(scratch),
            compiler_params=PARAMS,
            cost_estimate=pl.CostEstimate(flops=flops, bytes_accessed=4 * moved, transcendentals=0),
            name=name,
        )(*given)

    return run


def swap(x, sizes, blk=0, shard=0, sub=0):
    n_blk, n_shard, n_sub = sizes

    def number(b, k, u):
        return (b * n_shard + k) * n_sub + u

    route = [
        (number(b, k, u), number(b ^ blk, k ^ shard, u ^ sub))
        for b in range(n_blk)
        for k in range(n_shard)
        for u in range(n_sub)
    ]
    return lax.ppermute(x, AXES, route)


def sum_pieces(terms, sizes, width, kinds, beside=None, work=lambda _: ()):
    half = PIECES // 2
    piece = (piece_rows(width, kinds), LANES)
    sent = terms[half:]
    if beside is not None:
        sent, beside = lax.optimization_barrier((sent, beside))
        beside = from_behind(beside, "blk")
    other = swap(sent, sizes, sub=1)
    got = [
        swap(jnp.concatenate([terms[i], other[i]], axis=0), sizes, blk=i & 1, shard=i >> 1) for i in range(1, half)
    ]
    if beside is not None:
        got[1], beside = lax.optimization_barrier((got[1], beside))
    total = call(functools.partial(chip_kernel, width, kinds), [piece], name="chip_terms")(terms, other)[0]
    for more in (got[1], got[2], got[0]):
        total = call(functools.partial(more_kernel, width, kinds), [piece], name="more_terms")(total, more)[0]
    reach = 4
    while reach <= sizes[0]:
        total = total + swap(total, sizes, blk=reach - 1)
        reach *= 2
    reach = 4
    while reach <= sizes[1]:
        total = total + swap(total, sizes, shard=reach - 1)
        reach *= 2
    total, aside = lax.optimization_barrier((total, work(beside)))
    mine = [total] + [swap(total, sizes, blk=i & 1, shard=i >> 1) for i in range(1, half)]
    return mine + [swap(x, sizes, sub=1) for x in mine], beside, aside


def from_behind(block, axis):
    n = lax.axis_size(axis)
    return lax.ppermute(block, axis, [((i - 1) % n, i) for i in range(n)])


def shards(
    head_table, head_accum, tail_table, tail_accum, relations, rel_accum, head_ids, tail_ids, rel_ids, neg_ids
):
    sizes = tuple(lax.axis_size(a) for a in AXES)
    steps = head_ids.shape[0]
    rows, width = head_table.shape
    kinds = relations.shape[0]

    left, lacc = head_table.T, head_accum[None]
    rel, relacc = relations.T, rel_accum[None]
    edges = head_ids.shape[1]
    table, state, each = (width, rows), (1, rows), (width, edges)
    cut_terms = (PIECES, term_rows(width, edges), LANES)
    given = (head_ids, tail_ids, rel_ids, neg_ids, left, tail_table.T, tail_accum[None], rel)
    right, terms, carry = pl.pallas_call(
        first_kernel,
        out_shape=[jax.ShapeDtypeStruct(shape, F32) for shape in [(width + 8, rows), cut_terms, each]],
        in_specs=[HBM] * len(given),
        out_specs=[VMEM] * 3,
        scratch_shapes=[pltpu.VMEM(x.shape, x.dtype) for x in given] + [pltpu.SemaphoreType.DMA((len(given),))],
        compiler_params=PARAMS,
        name="first_step",
    )(*[pltpu.with_memory_space_constraint(x, pltpu.HBM) for x in given])
    all_pieces = pltpu.VMEM((PIECES, piece_rows(width, kinds), LANES), F32)
    half = PIECES // 2
    main, rest = cut(width)

    def short(*shape):
        return jax.ShapeDtypeStruct(shape, BF16)

    def relations(rel, relacc, summed, shape, name):
        return call(relations_kernel, [(width, kinds), shape], [all_pieces], name=name)(rel, relacc, *summed)

    summed = None
    for step in range(1, steps):
        if step > 1:
            right = call(right_kernel, [(width + 8, rows)])(right, query, weight)[0]

        def ready(right, step=step, rel=rel, relacc=relacc, summed=summed):
            if summed is not None:
                rel, relacc = relations(rel, relacc, summed, (1, kinds), "relations")
            outs = [table, state, each, short(2 * rows, width), short(2 * width, rows), (rows, edges), (rows, edges)]
            outs += [short(kinds, edges), each, (1, edges)]
            return rel, relacc, *call(functools.partial(ready_kernel, step), outs, name="ready")(
                left, lacc, carry, right, rel, relacc, head_ids, tail_ids, rel_ids, neg_ids
            )

        summed, right, (rel, relacc, left, lacc, heads, turned, both, named, tail_sel, kind_sel, rel_rows, rel_state) = (
            sum_pieces(terms, sizes, width, kinds, right, ready)
        )
        mine = call(functools.partial(gather_kernel, width), [(half * (main + rest), edges)], name="gather")(
            *summed[:half], kind_sel
        )[0]
        terms, carry, query, weight = call(
            functools.partial(next_kernel, step),
            [cut_terms, each, each, (rows, edges)],
            [pltpu.VMEM((PIECES, main, edges), F32), pltpu.VMEM((PIECES, 8, edges), F32)],
            name="next_step",
        )(heads, turned, both, named, tail_sel, kind_sel, rel_rows, rel_state, mine, *summed[half:], rel_ids)

    def update(_):
        return *relations(rel, relacc, summed, (1, kinds), "relations"), *call(
            functools.partial(update_kernel, steps - 1), [table, (rows,), table, (rows,)], name="last_update"
        )(left, lacc, carry, head_ids, right, query, weight)

    last, _, (rel, relacc, left, lacc, right, racc) = sum_pieces(terms, sizes, width, kinds, work=update)
    rel, relacc = relations(rel, relacc, last, (kinds,), "last_relations")
    return (left.T, lacc, right.T, racc, rel.T, relacc)


def solution(mesh):
    every = ("groups", "blk", "shard", "sub")
    return jax.shard_map(
        shards,
        mesh=mesh,
        in_specs=(
            P(every, None),
            P(every),
            P(every, None),
            P(every),
            P("groups", None),
            P("groups"),
            P(None, every),
            P(None, every),
            P(None, every),
            P(None, every, None),
        ),
        out_specs=(P(every, None), P(every), P(every, None), P(every), P("groups", None), P("groups")),
        check_vma=False,
    )
```

```python
import functools
import math

import jax
import jax.numpy as jnp
from jax import lax
from jax.experimental import pallas as pl
from jax.experimental.pallas import tpu as pltpu
from jax.sharding import PartitionSpec as P

RATE = 0.1
AXES = ("blk", "shard", "sub")
LANES = 128
PIECES = 8
F32 = jnp.float32
BF16 = jnp.bfloat16


def halves(x):
    high = x.astype(BF16)
    return high, (x - high.astype(F32)).astype(BF16)


def nn(a, b):
    return lax.dot_general(a, b, (((1,), (0,)), ((), ())), preferred_element_type=F32)


def nt(a, b):
    return lax.dot_general(a, b, (((1,), (1,)), ((), ())), preferred_element_type=F32)


def stack(x):
    high = x.astype(BF16).astype(F32)
    return jnp.concatenate([high, x - high], axis=0).astype(BF16)


def times_selector(dot, x, selector):
    rows = x.shape[0]
    both = dot(stack(x), selector)
    return both[:rows] + both[rows:]


def times(dot, a, b):
    a_high, a_low = halves(a)
    b_high, b_low = halves(b)
    rows = a.shape[0]
    both = dot(jnp.concatenate([a_high, a_low], axis=0), b_high)
    return both[:rows] + (both[rows:] + dot(a_high, b_low))


def selector(ids, rows):
    return (lax.broadcasted_iota(jnp.int32, (rows, ids.shape[1]), 0) == ids).astype(F32)


def adagrad(weights, accum, grads):
    accum = accum + jnp.sum(grads * grads, axis=0, keepdims=True) * (1.0 / grads.shape[0])
    return weights - grads * (RATE / jnp.sqrt(accum)), accum


def prepare(right, tail_ids, negative):
    rows = right.shape[1]
    count, negs = negative.shape
    named = []
    for c in range(count):
        hits = lax.broadcasted_iota(jnp.int32, (rows, negs), 0) == negative[c : c + 1]
        share = jnp.sum(hits.astype(F32), axis=1, keepdims=True) * (1.0 / negs)
        named.append(jnp.broadcast_to(share, (rows, tail_ids.shape[1] // count)))
    return jnp.concatenate(named, axis=1), selector(tail_ids, rows)


def split_times(dot, a_both, b):
    rows = a_both.shape[0] // 2
    b_high, b_low = halves(b)
    both = dot(a_both, b_high)
    return both[:rows] + (both[rows:] + dot(a_both[:rows], b_low))


def score(right_turned, query, named, tail_sel):
    scores = split_times(nn, right_turned, query)
    tiny = jnp.exp(-jnp.abs(scores))
    inverse = 1.0 / (1.0 + tiny)
    up = scores >= 0
    sig = jnp.where(up, 1.0, tiny) * inverse
    sig_minus = jnp.where(up, tiny, 1.0) * inverse
    return named * sig - tail_sel * sig_minus


def gray(i):
    return jnp.bitwise_and(jnp.bitwise_xor(i, i >> 1), 1)


def place():
    return gray(lax.axis_index("shard")) * 2 + gray(lax.axis_index("blk")), lax.axis_index("sub")


def cut(width):
    main = width // (8 * PIECES) * 8
    return main, width // PIECES - main


def piece_rows(width, kinds):
    return -(-(width // PIECES) * kinds // LANES // 8) * 8


def term_rows(width, edges):
    return edges // LANES * cut(width)[0] + 8


def put_terms(terms, kinds, out_ref):
    square, core = place()
    width, edges = terms.shape
    half = PIECES // 2
    main, rest = cut(width)
    tiles = [slice(LANES * j, LANES * (j + 1)) for j in range(edges // LANES)]
    ids = [kinds[:, lanes].astype(F32) for lanes in tiles]
    ids.append(jnp.zeros((8 - len(tiles) * (rest + 1), LANES), F32))
    for c in range(PIECES):
        at = jnp.bitwise_xor(c // half, core) * half + jnp.bitwise_xor(c % half, square)
        last = main * PIECES + rest * c
        for j, lanes in enumerate(tiles):
            out_ref[at, main * j : main * (j + 1)] = terms[main * c : main * (c + 1), lanes]
        out_ref[at, main * len(tiles) :] = jnp.concatenate(
            [terms[last : last + rest, lanes] for lanes in tiles] + ids, axis=0
        )


def turn(x, by):
    return [x[by:], x[:by]] if by else [x]


def sum_terms(width, kinds, parts):
    main, rest = cut(width)
    total = None
    for part in parts:
        tiles = part.shape[0] // main
        below = part[main * tiles :]
        each = [
            jnp.concatenate([part[main * j : main * (j + 1)]] + turn(below, rest * j), axis=0)
            for j in range(tiles)
        ]
        first = rest * tiles
        ids = jnp.concatenate([below[first + j : first + j + 1] for j in range(tiles)], axis=1)
        both = stack(jnp.concatenate(each, axis=1))
        grad = nt(both, selector(ids.astype(jnp.int32), kinds).astype(BF16))
        grad = grad[: main + 8] + grad[main + 8 :]
        total = grad if total is None else total + grad
    return total


def put_piece(grad, width, out_ref, before_ref=None):
    main, rest = cut(width)
    blocks = grad.shape[1] // LANES
    for j in range(blocks):
        lanes = slice(LANES * j, LANES * (j + 1))
        for rows, part in (
            (slice(main * j, main * (j + 1)), grad[:main, lanes]),
            (slice(main * blocks + rest * j, main * blocks + rest * (j + 1)), grad[main : main + rest, lanes]),
        ):
            out_ref[rows] = part if before_ref is None else before_ref[rows] + part
    end = (main + rest) * blocks
    out_ref[end:] = jnp.zeros((out_ref.shape[0] - end, LANES), F32)


def chip_kernel(width, kinds, own_ref, other_ref, out_ref):
    put_piece(sum_terms(width, kinds, [own_ref[0], other_ref[0]]), width, out_ref)


def more_kernel(width, kinds, total_ref, terms_ref, out_ref):
    rows = terms_ref.shape[0] // 2
    put_piece(sum_terms(width, kinds, [terms_ref[:rows], terms_ref[rows:]]), width, out_ref, total_ref)


def order_pieces(piece_refs, all_ref):
    square, core = place()
    half = PIECES // 2
    for i in range(half):
        piece = jnp.bitwise_xor(square, i)
        all_ref[core * half + piece] = piece_refs[i][...]
        all_ref[(1 - core) * half + piece] = piece_refs[half + i][...]


def take_rel_grad(all_ref, j, width, blocks):
    main, rest = cut(width)
    first, last = main * j, main * blocks + rest * j
    return jnp.concatenate(
        [all_ref[c, first : first + main] for c in range(PIECES)]
        + [all_ref[c, last : last + rest] for c in range(PIECES)],
        axis=0,
    )


def next_accum(relacc_ref, piece_refs, width):
    squares = []
    main, rest = cut(width)
    blocks = relacc_ref.shape[1] // LANES
    for j in range(blocks):
        tiles, rests = None, None
        for ref in piece_refs:
            whole = ref[main * j : main * (j + 1)].reshape(-1, 8, LANES)
            whole = jnp.sum(whole * whole, axis=0)
            first = main * blocks + rest * j
            below = ref[first : first + rest]
            below = below * below
            tiles = whole if tiles is None else tiles + whole
            rests = below if rests is None else rests + below
        squares.append(jnp.sum(tiles, axis=0, keepdims=True) + jnp.sum(rests, axis=0, keepdims=True))
    accum = relacc_ref[...] + jnp.concatenate(squares, axis=1) * (1.0 / width)
    return accum, RATE / jnp.sqrt(accum)


def put_packed(out_ref, right, acc):
    width = right.shape[0]
    out_ref[:width] = right
    out_ref[width:] = jnp.broadcast_to(acc, (8, acc.shape[1]))


def first_kernel(*refs):
    given, (right_out, terms_out, carry_out), held, sems = refs[:8], refs[8:11], refs[11:19], refs[19]
    copies = [pltpu.make_async_copy(a, b, sems.at[i]) for i, (a, b) in enumerate(zip(given, held))]
    for copy in copies:
        copy.start()
    hid_ref, tid_ref, kid_ref, nid_ref, left_ref, right_ref, racc_ref, rel_ref = held
    for copy in copies[:5]:
        copy.wait()
    head_sel = selector(hid_ref[0:1], left_ref.shape[1]).astype(BF16)
    kind_sel = selector(kid_ref[0:1], rel_ref.shape[1]).astype(BF16)
    heads = times_selector(nn, left_ref[...], head_sel)
    for copy in copies[5:]:
        copy.wait()
    right = right_ref[...]
    rel_rows = times_selector(nn, rel_ref[...], kind_sel)
    query = heads * rel_rows
    weight = score(stack(right.T), query, *prepare(right, tid_ref[0:1], nid_ref[0]))
    grad_query = times(nn, right, weight)
    put_terms(grad_query * heads, kid_ref[0:1], terms_out)
    put_packed(right_out, *adagrad(right, racc_ref[...], times(nt, query, weight)))
    carry_out[...] = grad_query * rel_rows


def ready_kernel(
    step, left_ref, lacc_ref, carry_ref, right_ref, rel_ref, relacc_ref, hid_ref, tid_ref, kid_ref, nid_ref,
    left_out, lacc_out, heads_out, turned_out, right_out, named_out, tail_out, kind_out, rows_out, state_out,
):
    width, rows = left_ref.shape
    grad = times_selector(nt, carry_ref[...], selector(hid_ref[step - 1 : step], rows).astype(BF16))
    left, lacc_out[...] = adagrad(left_ref[...], lacc_ref[...], grad)
    left_out[...] = left
    heads_out[...] = times_selector(nn, left, selector(hid_ref[step : step + 1], rows).astype(BF16))
    right = right_ref[:width]
    turned_out[...] = stack(right.T)
    right_out[...] = stack(right)
    named_out[...], tail_out[...] = prepare(right, tid_ref[step : step + 1], nid_ref[step])
    kind_sel = selector(kid_ref[step : step + 1], rel_ref.shape[1]).astype(BF16)
    kind_out[...] = kind_sel
    state = jnp.broadcast_to(relacc_ref[...], (8, rel_ref.shape[1]))
    rel_rows = times_selector(nn, jnp.concatenate([rel_ref[...], state], axis=0), kind_sel)
    rows_out[...] = rel_rows[:width]
    state_out[...] = rel_rows[width : width + 1]


def gather_pieces(piece_refs, kind_sel, width):
    main, rest = cut(width)
    blocks = kind_sel.shape[0] // LANES
    mains = [jnp.concatenate([ref[main * j : main * (j + 1)] for j in range(blocks)], axis=1) for ref in piece_refs]
    first = main * blocks
    rests = [
        jnp.concatenate([ref[first + rest * j : first + rest * (j + 1)] for j in range(blocks)], axis=1)
        for ref in piece_refs
    ]
    return times_selector(nn, jnp.concatenate(mains + rests, axis=0), kind_sel)


def gather_kernel(width, *refs):
    refs[-1][...] = gather_pieces(refs[:-2], refs[-2][...], width)


def next_kernel(step, heads_ref, turned_ref, right_ref, named_ref, tail_ref, kind_ref, rows_ref, *refs):
    state_ref, mine_ref, piece_refs, kid_ref = refs[0], refs[1], refs[2 : 2 + PIECES // 2], refs[2 + PIECES // 2]
    terms_out, carry_out, query_out, weight_out, main_ref, rest_ref = refs[3 + PIECES // 2 :]
    heads = heads_ref[...]
    width = heads.shape[0]
    square, core = place()
    half = PIECES // 2
    main, rest = cut(width)
    theirs = gather_pieces(piece_refs, kind_ref[...], width)
    for first, columns in ((core * half, mine_ref[...]), ((1 - core) * half, theirs)):
        for i in range(half):
            at = first + jnp.bitwise_xor(square, i)
            last = main * half + rest * i
            main_ref[at] = columns[main * i : main * (i + 1)]
            rest_ref[at, :rest] = columns[last : last + rest]
    grad = jnp.concatenate([main_ref[c] for c in range(PIECES)] + [rest_ref[c, :rest] for c in range(PIECES)], axis=0)
    state = state_ref[...] + jnp.sum(grad * grad, axis=0, keepdims=True) * (1.0 / width)
    rel_rows = rows_ref[...] - grad * (RATE / jnp.sqrt(state))
    query = heads * rel_rows
    weight = score(turned_ref[...], query, named_ref[...], tail_ref[...])
    grad_query = split_times(nn, right_ref[...], weight)
    put_terms(grad_query * heads, kid_ref[step : step + 1], terms_out)
    carry_out[...] = grad_query * rel_rows
    query_out[...] = query
    weight_out[...] = weight


def relations_kernel(rel_ref, relacc_ref, *refs):
    piece_refs, (rel_out, relacc_out, all_ref) = refs[:PIECES], refs[PIECES:]
    width = rel_ref.shape[0]
    order_pieces(piece_refs, all_ref)
    accum, rate = next_accum(relacc_ref, piece_refs, width)
    relacc_out[...] = accum[0] if len(relacc_out.shape) == 1 else accum
    blocks = rel_ref.shape[1] // LANES
    for j in range(blocks):
        lanes = slice(LANES * j, LANES * (j + 1))
        rel_out[:, lanes] = rel_ref[:, lanes] - take_rel_grad(all_ref, j, width, blocks) * rate[:, lanes]


def right_kernel(right_ref, query_ref, weight_ref, right_out):
    width = query_ref.shape[0]
    grad = times(nt, query_ref[...], weight_ref[...])
    put_packed(right_out, *adagrad(right_ref[:width], right_ref[width : width + 1], grad))


def update_kernel(
    step, left_ref, lacc_ref, carry_ref, hid_ref, right_ref, query_ref, weight_ref,
    left_out, lacc_out, right_out, racc_out,
):
    rows = left_ref.shape[1]
    grad = times_selector(nt, carry_ref[...], selector(hid_ref[step : step + 1], rows).astype(BF16))
    left_out[...], acc = adagrad(left_ref[...], lacc_ref[...], grad)
    lacc_out[...] = acc[0]
    width = left_ref.shape[0]
    grad = times(nt, query_ref[...], weight_ref[...])
    right_out[...], acc = adagrad(right_ref[:width], right_ref[width : width + 1], grad)
    racc_out[...] = acc[0]


HBM = pl.BlockSpec(memory_space=pltpu.HBM)
VMEM = pl.BlockSpec(memory_space=pltpu.VMEM)
PARAMS = pltpu.CompilerParams(vmem_limit_bytes=40 * 1024 * 1024)


def call(kernel, outs, scratch=(), hbm_outs=(), name=None, flops=0):
    def run(*given):
        moved = sum(math.prod(x.shape) for x in given) + sum(math.prod(getattr(shape, "shape", shape)) for shape in outs)
        return pl.pallas_call(
            kernel,
            out_shape=[jax.ShapeDtypeStruct(shape, F32) if isinstance(shape, tuple) else shape for shape in outs],
            in_specs=[VMEM] * len(given),
            out_specs=[HBM if i in hbm_outs else VMEM for i in range(len(outs))],
            scratch_shapes=list(scratch),
            compiler_params=PARAMS,
            cost_estimate=pl.CostEstimate(flops=flops, bytes_accessed=4 * moved, transcendentals=0),
            name=name,
        )(*given)

    return run


def swap(x, sizes, blk=0, shard=0, sub=0):
    n_blk, n_shard, n_sub = sizes

    def number(b, k, u):
        return (b * n_shard + k) * n_sub + u

    route = [
        (number(b, k, u), number(b ^ blk, k ^ shard, u ^ sub))
        for b in range(n_blk)
        for k in range(n_shard)
        for u in range(n_sub)
    ]
    return lax.ppermute(x, AXES, route)


def sum_pieces(terms, sizes, width, kinds, beside=None, work=lambda _: ()):
    half = PIECES // 2
    piece = (piece_rows(width, kinds), LANES)
    sent = terms[half:]
    if beside is not None:
        sent, beside = lax.optimization_barrier((sent, beside))
        beside = from_behind(beside, "blk")
    other = swap(sent, sizes, sub=1)
    got = [
        swap(jnp.concatenate([terms[i], other[i]], axis=0), sizes, blk=i & 1, shard=i >> 1) for i in range(1, half)
    ]
    if beside is not None:
        got[1], beside = lax.optimization_barrier((got[1], beside))
    total = call(functools.partial(chip_kernel, width, kinds), [piece], name="chip_terms")(terms, other)[0]
    for more in (got[1], got[2], got[0]):
        total = call(functools.partial(more_kernel, width, kinds), [piece], name="more_terms")(total, more)[0]
    reach = 4
    while reach <= sizes[0]:
        total = total + swap(total, sizes, blk=reach - 1)
        reach *= 2
    reach = 4
    while reach <= sizes[1]:
        total = total + swap(total, sizes, shard=reach - 1)
        reach *= 2
    total, aside = lax.optimization_barrier((total, work(beside)))
    mine = [total] + [swap(total, sizes, blk=i & 1, shard=i >> 1) for i in range(1, half)]
    return mine + [swap(x, sizes, sub=1) for x in mine], beside, aside


def from_behind(block, axis):
    n = lax.axis_size(axis)
    return lax.ppermute(block, axis, [((i - 1) % n, i) for i in range(n)])


def shards(
    head_table, head_accum, tail_table, tail_accum, relations, rel_accum, head_ids, tail_ids, rel_ids, neg_ids
):
    sizes = tuple(lax.axis_size(a) for a in AXES)
    steps = head_ids.shape[0]
    rows, width = head_table.shape
    kinds = relations.shape[0]

    left, lacc = head_table.T, head_accum[None]
    rel, relacc = relations.T, rel_accum[None]
    edges = head_ids.shape[1]
    table, state, each = (width, rows), (1, rows), (width, edges)
    cut_terms = (PIECES, term_rows(width, edges), LANES)
    given = (head_ids, tail_ids, rel_ids, neg_ids, left, tail_table.T, tail_accum[None], rel)
    right, terms, carry = pl.pallas_call(
        first_kernel,
        out_shape=[jax.ShapeDtypeStruct(shape, F32) for shape in [(width + 8, rows), cut_terms, each]],
        in_specs=[HBM] * len(given),
        out_specs=[VMEM] * 3,
        scratch_shapes=[pltpu.VMEM(x.shape, x.dtype) for x in given] + [pltpu.SemaphoreType.DMA((len(given),))],
        compiler_params=PARAMS,
        name="first_step",
    )(*[pltpu.with_memory_space_constraint(x, pltpu.HBM) for x in given])
    all_pieces = pltpu.VMEM((PIECES, piece_rows(width, kinds), LANES), F32)
    half = PIECES // 2
    main, rest = cut(width)

    def short(*shape):
        return jax.ShapeDtypeStruct(shape, BF16)

    def relations(rel, relacc, summed, shape, name):
        return call(relations_kernel, [(width, kinds), shape], [all_pieces], name=name)(rel, relacc, *summed)

    summed = None
    for step in range(1, steps):
        if step > 1:
            right = call(right_kernel, [(width + 8, rows)])(right, query, weight)[0]

        def ready(right, step=step, rel=rel, relacc=relacc, summed=summed):
            if summed is not None:
                rel, relacc = relations(rel, relacc, summed, (1, kinds), "relations")
            outs = [table, state, each, short(2 * rows, width), short(2 * width, rows), (rows, edges), (rows, edges)]
            outs += [short(kinds, edges), each, (1, edges)]
            return rel, relacc, *call(functools.partial(ready_kernel, step), outs, name="ready")(
                left, lacc, carry, right, rel, relacc, head_ids, tail_ids, rel_ids, neg_ids
            )

        summed, right, (rel, relacc, left, lacc, heads, turned, both, named, tail_sel, kind_sel, rel_rows, rel_state) = (
            sum_pieces(terms, sizes, width, kinds, right, ready)
        )
        mine = call(functools.partial(gather_kernel, width), [(half * (main + rest), edges)], name="gather")(
            *summed[:half], kind_sel
        )[0]
        terms, carry, query, weight = call(
            functools.partial(next_kernel, step),
            [cut_terms, each, each, (rows, edges)],
            [pltpu.VMEM((PIECES, main, edges), F32), pltpu.VMEM((PIECES, 8, edges), F32)],
            name="next_step",
        )(heads, turned, both, named, tail_sel, kind_sel, rel_rows, rel_state, mine, *summed[half:], rel_ids)

    def update(_):
        return *relations(rel, relacc, summed, (1, kinds), "relations"), *call(
            functools.partial(update_kernel, steps - 1), [table, (rows,), table, (rows,)], name="last_update"
        )(left, lacc, carry, head_ids, right, query, weight)

    last, _, (rel, relacc, left, lacc, right, racc) = sum_pieces(terms, sizes, width, kinds, work=update)
    rel, relacc = relations(rel, relacc, last, (kinds,), "last_relations")
    return (left.T, lacc, right.T, racc, rel.T, relacc)


def solution(mesh):
    every = ("groups", "blk", "shard", "sub")
    return jax.shard_map(
        shards,
        mesh=mesh,
        in_specs=(
            P(every, None),
            P(every),
            P(every, None),
            P(every),
            P("groups", None),
            P("groups"),
            P(None, every),
            P(None, every),
            P(None, every),
            P(None, every, None),
        ),
        out_specs=(P(every, None), P(every), P(every, None), P(every), P("groups", None), P("groups")),
        check_vma=False,
    )
```
